256 devices in a mesh: cols: 32 (over z, y), lev: 8 (over x, core).
Axes of the slice: x: 4, y: 4, z: 8, core: 2. Of those that a mesh axis runs over, the one named last changes fastest.
Arguments:
- departures: float32 [128, 1015808], P('lev', 'cols'), may hold values from -6 to 6
- restrict_offset: int32 [8, 32768], P(None, 'cols'), may hold values from -8192 to 8192, as said below
- restrict_weight: float32 [8, 32768], P(None, 'cols'), may hold values from 0.05 to 0.3
- correlation_count: int32 [32768], P('cols'), may hold values from 1 to 8
- increment: float32 [128, 32768], P('lev', 'cols'), may hold values from -7 to 7
- center: float32 [128, 32768], P('lev', 'cols'), may hold values from 1 to 2
- vertical_coupling: float32 [128, 32768], P('lev', 'cols'), may hold values from -0.4 to 0.4
- neighbors: int32 [4, 32768], P(None, 'cols'), may hold values from 0 to 32767, as said below
- couple: float32 [4, 32768], P(None, 'cols'), may hold values from -0.4 to 0.4
- step_pairs: bfloat16 [4, 128, 32768], P(None, 'lev', 'cols'), may hold values from -13 to 13
- grad_pairs: bfloat16 [4, 128, 32768], P(None, 'lev', 'cols'), may hold values from -30 to 30, as said below
Outputs:
- gradient: float32 [128, 32768], P('lev', 'cols')
- direction: float32 [128, 32768], P('lev', 'cols')
The draws below stay inside these ranges and needn't reach their ends.
Inputs may be any that keep to these rules, and one draw needn't show every extreme that they name: Entry k of coarse column j's correlation list is the fine column (31 j + restrict_offset[k, j]) modulo 1015808. `neighbors`: rows are the columns j - 1, j + 1, j - a and j + b modulo 32768, with a and b between 1 and 512. grad_pairs is step_pairs times a factor between 0.2 and 2.3 in each entry.
All inputs are finite; a program needn't handle non-finite values.
Results may differ from the reference program's by a relative error of at most 0.0003.
Values sent between devices are 32-bit elements; how exact they have to be, the bound alone decides.
A program may use at most 128 MiB of HBM per device.

```python
import jax
import jax.numpy as jnp

RATIO = 31
K = 8
M = 4
HALO_F = 8192
HALO_C = 512
LEVELS = 128
NCOARSE = 32768
NFINE = 1015808


def shared_base(key):
    normal_key = jax.random.fold_in(key, 0)
    normal_part = jnp.clip(jax.random.normal(normal_key, (LEVELS, NCOARSE), jnp.float32), -4.0, 4.0)
    return normal_part


def pair_fields(key):
    base = shared_base(key)
    key = jax.random.fold_in(key, 101)
    coef_key = jax.random.fold_in(key, 0)
    sign_key = jax.random.fold_in(key, 1)
    normal_key = jax.random.fold_in(key, 2)
    factor_key = jax.random.fold_in(key, 4)
    jitter_key = jax.random.fold_in(key, 5)
    coefs = jax.random.uniform(coef_key, (M, 1, 1), jnp.float32, 0.5, 1.5)
    signs = jnp.where(jax.random.bernoulli(sign_key, 0.5, (M, 1, 1)), 1.0, -1.0)
    normal_noise = jnp.clip(jax.random.normal(normal_key, (M, LEVELS, NCOARSE), jnp.float32), -4.0, 4.0)
    noise = normal_noise
    step_field = signs * coefs * base[None, :, :] + noise
    factor = jax.random.uniform(factor_key, (M, LEVELS, NCOARSE), jnp.float32, 0.5, 2.0)
    jitter = jax.random.uniform(jitter_key, (M, LEVELS, NCOARSE), jnp.float32, -1.0, 1.0)
    return (step_field, step_field * (factor + 0.3 * jitter))


def draw_increment(key, part):
    return shared_base(key)


def draw_step_pairs(key, part):
    step_field, grad_field = pair_fields(key)
    return step_field.astype(jnp.bfloat16)


def draw_grad_pairs(key, part):
    step_field, grad_field = pair_fields(key)
    return grad_field.astype(jnp.bfloat16)


def draw_restrict_offset(key, part):
    key = jax.random.fold_in(key, 11)
    offsets = jax.random.randint(key, (K, NCOARSE), -HALO_F, HALO_F + 1, dtype=jnp.int32)
    offsets = offsets.at[0, 0].set(HALO_F).at[1, 0].set(-HALO_F)
    return offsets.astype(jnp.int32)


def draw_neighbors(key, part):
    key = jax.random.fold_in(key, 23)
    reaches = jax.random.randint(key, (2, NCOARSE), 1, HALO_C + 1, dtype=jnp.int32)
    reaches = reaches.at[0, 0].set(HALO_C).at[1, 0].set(HALO_C)
    columns = jnp.arange(NCOARSE, dtype=jnp.int32)
    rows = jnp.stack([columns - 1, columns + 1, columns - reaches[0], columns + reaches[1]])
    return (rows % NCOARSE).astype(jnp.int32)


def place_ends(result, own_key, low, largest):
    longest = result.shape.index(max(result.shape))
    spots = []
    for shift in (0, 1):
        where = [jax.random.randint(jax.random.fold_in(own_key, axis), (), 0, length) for axis, length in enumerate(result.shape)]
        where[longest] = (where[longest] + shift) % result.shape[longest]
        spots.append(tuple(where))
    return result.at[spots[0]].set(low).at[spots[1]].set(largest)


def block_scale(key, dims, cuts, smallest, high):
    level, own = 1.0, jax.random.fold_in(key, 6)
    for dim, shards_of in cuts:
        draws = jnp.exp(jax.random.uniform(jax.random.fold_in(own, dim), (shards_of,), jnp.float32, smallest / len(cuts), high / len(cuts)))
        level = level * jnp.repeat(draws, dims[dim] // shards_of).reshape([-1 if axis == dim else 1 for axis in range(len(dims))])
    return level


def normal_values(stream_key, shape, scale, reach, cuts=(), kind=jnp.bfloat16):
    gain = block_scale(stream_key, shape, cuts, -0.22, 0.18) if cuts else 1.0
    drawn = jax.random.normal(stream_key, shape, jnp.float32) * scale * gain
    return jnp.minimum(jnp.maximum(drawn, -reach), reach).astype(kind)


def setup_inputs(seed: int = 0) -> dict:
    streams_of = jax.random.split(jax.random.key(seed), 12)
    departures = normal_values(streams_of[0], (LEVELS, NFINE), 1.0, 6.0, ((0, 8), (1, 32)), jnp.float32)
    restrict_offset = draw_restrict_offset(jax.random.fold_in(streams_of[11], 71), 0)
    restrict_weight = jnp.clip(0.05 + 0.25 * jax.random.uniform(streams_of[2], (K, NCOARSE), jnp.float32) ** block_scale(streams_of[2], (K, NCOARSE), ((1, 32),), -0.2, 0.2), 0.05, 0.3)
    correlation_count = place_ends(jax.random.randint(streams_of[3], (NCOARSE,), 1, K + 1), jax.random.fold_in(streams_of[3], 1), 1, K).astype(jnp.int32)
    increment = draw_increment(jax.random.fold_in(streams_of[11], 71), 0)
    center = jnp.clip(1.0 + 1.0 * jax.random.uniform(streams_of[5], (LEVELS, NCOARSE), jnp.float32) ** block_scale(streams_of[5], (LEVELS, NCOARSE), ((0, 8), (1, 32)), -0.2, 0.2), 1.0, 2.0)
    vertical_coupling = jnp.clip(jax.random.uniform(streams_of[6], (LEVELS, NCOARSE), jnp.float32, -0.4, 0.4) * block_scale(streams_of[6], (LEVELS, NCOARSE), ((0, 8), (1, 32)), -0.4, 0.0), -0.4, 0.4)
    neighbors = draw_neighbors(jax.random.fold_in(streams_of[11], 71), 0)
    couple = jnp.clip(jax.random.uniform(streams_of[8], (4, NCOARSE), jnp.float32, -0.4, 0.4) * block_scale(streams_of[8], (4, NCOARSE), ((1, 32),), -0.4, 0.0), -0.4, 0.4)
    step_pairs = draw_step_pairs(jax.random.fold_in(streams_of[11], 71), 0)
    grad_pairs = draw_grad_pairs(jax.random.fold_in(streams_of[11], 71), 0)
    return dict(departures=departures, restrict_offset=restrict_offset, restrict_weight=restrict_weight, correlation_count=correlation_count, increment=increment, center=center, vertical_coupling=vertical_coupling, neighbors=neighbors, couple=couple, step_pairs=step_pairs, grad_pairs=grad_pairs)


def vertical_term(column_field, vertical_coupling):
    zeros_row = jnp.zeros((1, column_field.shape[1]), jnp.float32)
    upper = jnp.concatenate([column_field[1:], zeros_row], axis=0)
    lower = jnp.concatenate([zeros_row, column_field[:-1]], axis=0)
    lower_coupling = jnp.concatenate([zeros_row, vertical_coupling[:-1]], axis=0)
    return vertical_coupling * upper + lower_coupling * lower


def reference(departures, restrict_offset, restrict_weight, correlation_count, increment, center, vertical_coupling, neighbors, couple, step_pairs, grad_pairs):
    columns = jnp.arange(NCOARSE, dtype=jnp.int32)
    restricted = jnp.zeros(increment.shape, jnp.float32)
    for entry in range(K):
        weight_row = jnp.where(entry < correlation_count, restrict_weight[entry], jnp.float32(0.0))
        fine_index = ((RATIO * columns + restrict_offset[entry]) % NFINE).astype(jnp.int32)
        restricted = restricted + weight_row[None, :] * jnp.take(departures, fine_index, axis=1)
    image = center * increment + vertical_term(increment, vertical_coupling)
    for side in range(4):
        image = image + couple[side][None, :] * jnp.take(increment, neighbors[side], axis=1)
    misfit = image - restricted
    adjoint = center * misfit + vertical_term(misfit, vertical_coupling)
    for side in range(4):
        adjoint = adjoint.at[:, neighbors[side]].add(couple[side][None, :] * misfit)
    gradient = increment + adjoint
    inverses = []
    for pair in range(M):
        inverses.append(1.0 / jnp.sum(step_pairs[pair].astype(jnp.float32) * grad_pairs[pair].astype(jnp.float32)))
    current = gradient
    alphas = [None] * M
    for pair in range(M - 1, -1, -1):
        alphas[pair] = inverses[pair] * jnp.sum(step_pairs[pair].astype(jnp.float32) * current)
        current = current - alphas[pair] * grad_pairs[pair].astype(jnp.float32)
    last_step = step_pairs[M - 1].astype(jnp.float32)
    last_grad = grad_pairs[M - 1].astype(jnp.float32)
    scaling = jnp.sum(last_step * last_grad) / jnp.sum(last_grad * last_grad)
    current = scaling * current
    for pair in range(M):
        betas = inverses[pair] * jnp.sum(grad_pairs[pair].astype(jnp.float32) * current)
        current = current + (alphas[pair] - betas) * step_pairs[pair].astype(jnp.float32)
    return gradient, -current
```

```python
import functools

import jax
import jax.numpy as jnp
from jax import lax
from jax.experimental import pallas as pl
from jax.experimental.pallas import tpu as pltpu
from jax.sharding import PartitionSpec as P

K = 8
M = 4
RATIO = 31
ROWS = 16
COLS = 1024
FINE = RATIO * COLS
SEG = 4096
HALO = 512
EXT = COLS + 2 * HALO
EDGE = 384
OWN = COLS // 128
FOREIGN = 2 * EDGE // 128
UNROLL = 16
WIDE = 256
REACH = WIDE + HALO
NY = 4
F32 = jnp.float32
I32 = jnp.int32
BF16 = jnp.bfloat16


def halves(value):
    high = value.astype(BF16)
    low = (value - high.astype(F32)).astype(BF16)
    return jnp.concatenate([high, low], axis=0)


def lane_sums(value):
    total = value[0:8] + value[8:16]
    parts = [total[:, 128 * i : 128 * i + 128] for i in range(COLS // 128)]
    while len(parts) > 1:
        parts = [parts[i] + parts[i + 1] for i in range(0, len(parts), 2)]
    return jnp.sum(parts[0], axis=0, keepdims=True)


def kernel(
    tiles,
    slabs,
    dep_hbm,
    off_hbm,
    wgt_hbm,
    cnt_hbm,
    inc_hbm,
    cen_hbm,
    vc_hbm,
    nbr_hbm,
    cpl_hbm,
    step_hbm,
    grad_hbm,
    gradient_ref,
    direction_ref,
    dep,
    off,
    wgt,
    cnt,
    cen,
    vc,
    nbr,
    cpl,
    steps,
    grads,
    fine,
    table,
    acc,
    f_own,
    w_own,
    r_own,
    f_out,
    w_out,
    f_for,
    w_for,
    r_for,
    idx_own,
    idx_for,
    inc,
    parts,
    onehot,
    up_out,
    below,
    down_out,
    above,
    sum_out,
    sum_in,
    restricted,
    mis_out,
    mis_in,
    spread,
    rim_in,
    prods,
    red_lev,
    red_y,
    red_z,
    local_sem,
    send_sem,
    recv_sem,
    lev_send,
    lev_recv,
    y_send,
    y_recv,
    z_send,
    z_recv,
):
    tile = lax.axis_index("cols")
    slab = lax.axis_index("lev")
    nz = tiles // NY
    row_z = tile // NY
    row_y = lax.rem(tile, NY)
    left = lax.rem(tile + tiles - 1, tiles)
    right = lax.rem(tile + 1, tiles)
    lower = lax.rem(slab + slabs - 1, slabs)
    upper = lax.rem(slab + 1, slabs)

    def spot(column, level):
        return {"cols": column, "lev": level}

    lev_peers = [spot(tile, lax.rem(slab + d, slabs)) for d in range(1, slabs)]
    y_peers = [spot(row_z * NY + lax.rem(row_y + d, NY), slab) for d in range(1, NY)]
    z_peers = [spot(lax.rem(row_z + d, nz) * NY + row_y, slab) for d in range(1, nz)]

    def send(src, dst, i, target):
        copy = pltpu.make_async_remote_copy(
            src_ref=src,
            dst_ref=dst,
            send_sem=send_sem.at[i],
            recv_sem=recv_sem.at[i],
            device_id=target,
            device_id_type=pl.DeviceIdType.MESH,
        )
        copy.start()
        return copy

    loads = []
    for i, (src, dst) in enumerate(
        [
            (off_hbm, off),
            (wgt_hbm, wgt),
            (cnt_hbm, cnt),
            (inc_hbm, inc.at[:, HALO : HALO + COLS]),
            (vc_hbm, vc),
            (dep_hbm, dep),
            (nbr_hbm, nbr),
            (cpl_hbm, cpl),
            (cen_hbm, cen),
            (step_hbm, steps),
            (grad_hbm, grads),
        ]
    ):
        copy = pltpu.make_async_copy(src, dst, local_sem.at[i])
        copy.start()
        loads.append(copy)

    barrier = pltpu.get_barrier_semaphore()
    greeted = lev_peers + y_peers + z_peers + [spot(left, slab), spot(right, slab)]
    for peer in greeted:
        pl.semaphore_signal(barrier, inc=1, device_id=peer, device_id_type=pl.DeviceIdType.MESH)

    for i in range(5):
        loads[i].wait()

    lane = lax.broadcasted_iota(I32, (8, 128), 1)
    entry = lax.broadcasted_iota(I32, (8, 128), 0)
    for b in range(OWN):
        cut = slice(128 * b, 128 * b + 128)
        f = RATIO * (128 * b + lane) + off[:, cut]
        w = jnp.where(entry < cnt[:, cut], wgt[:, cut], 0.0)
        here = (f >= 0) & (f < FINE)
        fo = jnp.where(here, f, 0)
        f_own[b] = fo
        r_own[b] = fo & (SEG - 1)
        w_own[b] = jnp.where(here, w, 0.0)
        if b < FOREIGN // 2:
            f_out[b] = jnp.where(f < 0, f + FINE, 0)
            w_out[b] = jnp.where(f < 0, w, 0.0)
        if b >= OWN - FOREIGN // 2:
            at = b - OWN + FOREIGN
            f_out[at] = jnp.where(f >= FINE, f - FINE, 0)
            w_out[at] = jnp.where(f >= FINE, w, 0.0)
    own_index = pltpu.make_async_copy(r_own, idx_own, local_sem.at[11])
    own_index.start()
    up_out[0:1, :] = inc[ROWS - 1 : ROWS, HALO : HALO + COLS]
    up_out[1:2, :] = vc[ROWS - 1 : ROWS, :]
    down_out[...] = inc[0:1, HALO : HALO + COLS]

    pl.semaphore_wait(barrier, len(greeted))

    half = FOREIGN // 2
    to_left, to_right = spot(left, slab), spot(right, slab)
    to_lower, to_upper = spot(tile, lower), spot(tile, upper)
    lists = [
        send(f_out.at[0:half], f_for.at[0:half], 0, to_left),
        send(w_out.at[0:half], w_for.at[0:half], 1, to_left),
        send(f_out.at[half:FOREIGN], f_for.at[half:FOREIGN], 2, to_right),
        send(w_out.at[half:FOREIGN], w_for.at[half:FOREIGN], 3, to_right),
    ]
    halos = [
        send(inc.at[:, HALO : 2 * HALO], inc.at[:, HALO + COLS : EXT], 4, to_left),
        send(inc.at[:, COLS : COLS + HALO], inc.at[:, 0:HALO], 5, to_right),
        send(up_out, below, 6, to_upper),
        send(down_out, above, 7, to_lower),
    ]

    loads[5].wait()
    last = FINE // SEG
    tail = FINE - last * SEG
    for b in range(SEG // 128):
        pieces = [dep[:, SEG * g + 128 * b : SEG * g + 128 * b + 128] for g in range(last)]
        if 128 * b < tail:
            pieces.append(dep[:, SEG * last + 128 * b : SEG * last + 128 * b + 128])
        else:
            pieces.append(jnp.zeros((ROWS, 128), F32))
        fine[128 * b : 128 * b + 128, :] = jnp.concatenate(pieces, axis=0).T

    group = (lax.broadcasted_iota(I32, (128, 128), 1) // ROWS).astype(F32)

    def tabulate(f_ref, w_ref, base):
        def body(b, carry):
            packed = jnp.concatenate([w_ref[b], (f_ref[b] // SEG).astype(F32)], axis=0).T
            for k in range(K):
                weights = jnp.where(packed[:, K + k : K + k + 1] == group, packed[:, k : k + 1], 0.0)
                row = pl.multiple_of((base + b) * (K * 128) + k * 128, 128)
                table[pl.ds(row, 128), :] = weights
            return carry

        return body

    def gather(idx_ref, base):
        def body(t, carry):
            b = t // (128 // UNROLL)
            first = lax.rem(t, 128 // UNROLL) * UNROLL
            for u in range(UNROLL):
                terms = []
                for k in range(K):
                    at = idx_ref[b, k, first + u]
                    row = (base + b) * (K * 128) + k * 128 + first + u
                    terms.append(fine[pl.ds(at, 1), :] * table[pl.ds(row, 1), :])
                while len(terms) > 1:
                    terms = [terms[i] + terms[i + 1] for i in range(0, len(terms), 2)]
                acc[pl.ds((base + b) * 128 + first + u, 1), :] = terms[0]
            return carry

        return body

    def folded(b):
        flat = acc[128 * b : 128 * b + 128, :].T
        total = flat[0:ROWS]
        for g in range(1, 128 // ROWS):
            total = total + flat[ROWS * g : ROWS * g + ROWS]
        return total

    per = 128 // UNROLL
    lax.fori_loop(0, OWN, tabulate(f_own, w_own, 0), 0)
    own_index.wait()
    ahead = 24
    lax.fori_loop(0, ahead, gather(idx_own, 0), 0)

    for copy in lists:
        copy.wait()
    for b in range(FOREIGN):
        r_for[b] = f_for[b] & (SEG - 1)
    for_index = pltpu.make_async_copy(r_for, idx_for, local_sem.at[12])
    for_index.start()
    lax.fori_loop(0, FOREIGN, tabulate(f_for, w_for, OWN), 0)
    acc[(OWN + half - 1) * 128 : (OWN + half + 1) * 128, :] = jnp.zeros((256, 128), F32)
    for_index.wait()
    lax.fori_loop(0, 2 * per + 1, gather(idx_for, OWN), 0)
    for b in range(half):
        sum_out[0, :, 128 * b : 128 * b + 128] = folded(OWN + b)
    sums = [send(sum_out.at[0], sum_in.at[0], 8, to_right)]
    lax.fori_loop((half + 1) * per - 1, FOREIGN * per, gather(idx_for, OWN), 0)
    for b in range(half):
        sum_out[1, :, 128 * b : 128 * b + 128] = folded(OWN + half + b)
    sums.append(send(sum_out.at[1], sum_in.at[1], 9, to_left))

    lax.fori_loop(ahead, OWN * per, gather(idx_own, 0), 0)
    for b in range(OWN):
        restricted[:, 128 * b : 128 * b + 128] = folded(b)

    for i in range(6, 9):
        loads[i].wait()
    spots = (nbr[...] - tile * COLS + HALO) & (tiles * COLS - 1)
    for side in range(2):
        for b in range(COLS // WIDE):
            where = spots[2 + side : 3 + side, WIDE * b : WIDE * b + WIDE] - (WIDE * b + HALO * side)
            hit = lax.broadcasted_iota(I32, (REACH, WIDE), 0) == where
            onehot[side, b] = jnp.where(hit, 1.0, 0.0).astype(BF16)

    for copy in halos:
        copy.wait()
    parts[...] = halves(inc[...])
    mid = inc[:, HALO : HALO + COLS]
    row = lax.broadcasted_iota(I32, (ROWS, COLS), 0)
    couplings = vc[...]
    below_row = jnp.where(slab > 0, below[0:1, :], 0.0)
    below_coupling = jnp.where(slab > 0, below[1:2, :], 0.0)
    above_row = jnp.where(slab < slabs - 1, above[...], 0.0)
    couplings_down = jnp.where(row == 0, below_coupling, pltpu.roll(couplings, 1, 0))

    def vertical(value, under, over):
        up = jnp.where(row == ROWS - 1, over, pltpu.roll(value, ROWS - 1, 0))
        down = jnp.where(row == 0, under, pltpu.roll(value, 1, 0))
        return couplings * up + couplings_down * down

    image = cen[...] * mid + vertical(mid, below_row, above_row)
    around = inc[:, HALO - 128 : HALO + COLS + 128]
    image = image + cpl[0:1, :] * pltpu.roll(around, 1, 1)[:, 128 : 128 + COLS]
    image = image + cpl[1:2, :] * pltpu.roll(around, COLS + 255, 1)[:, 128 : 128 + COLS]
    blocks = []
    for b in range(COLS // WIDE):
        total = None
        for side in range(2):
            start = WIDE * b + HALO * side
            got = jnp.dot(parts[:, start : start + REACH], onehot[side, b], preferred_element_type=F32)
            term = cpl[2 + side : 3 + side, WIDE * b : WIDE * b + WIDE] * (got[0:ROWS] + got[ROWS : 2 * ROWS])
            total = term if total is None else total + term
        blocks.append(total)
    image = image + jnp.concatenate(blocks, axis=1)

    for i in range(9, 11):
        loads[i].wait()
    prods[...] = jnp.zeros((128, 128), F32)
    slot = {}
    for i in range(M):
        y_i = grads[i].astype(F32)
        s_i = steps[i].astype(F32)
        for j in range(i, M):
            y_j = grads[j].astype(F32)
            for name, value in (("sy", s_i), ("yy", y_i)):
                slot[name, i, j] = len(slot)
                at = slot[name, i, j]
                prods[at : at + 1, :] = lane_sums(value * y_j)

    for copy in sums:
        copy.wait()
    restricted[:, 0:EDGE] = restricted[:, 0:EDGE] + sum_in[0]
    restricted[:, COLS - EDGE : COLS] = restricted[:, COLS - EDGE : COLS] + sum_in[1]
    misfit = image - restricted[...]
    mis_out[0] = misfit[ROWS - 1 : ROWS, :]
    mis_out[1] = misfit[0:1, :]
    edges = [
        send(mis_out.at[0], mis_in.at[0], 10, to_upper),
        send(mis_out.at[1], mis_in.at[1], 11, to_lower),
    ]

    spread[...] = jnp.zeros((ROWS, EXT), F32)
    blank = jnp.zeros((ROWS, 128), F32)
    back = jnp.concatenate([blank, cpl[0:1, :] * misfit, blank], axis=1)
    forth = jnp.concatenate([blank, cpl[1:2, :] * misfit, blank], axis=1)
    spread[:, HALO - 128 : HALO + COLS + 128] = pltpu.roll(back, COLS + 255, 1) + pltpu.roll(forth, 1, 1)
    for b in range(COLS // WIDE):
        for side in range(2):
            start = WIDE * b + HALO * side
            carried = halves(cpl[2 + side : 3 + side, WIDE * b : WIDE * b + WIDE] * misfit[:, WIDE * b : WIDE * b + WIDE])
            out = lax.dot_general(
                carried, onehot[side, b], (((1,), (1,)), ((), ())), preferred_element_type=F32
            )
            spread[:, start : start + REACH] = spread[:, start : start + REACH] + (out[0:ROWS] + out[ROWS : 2 * ROWS])
    rims = [
        send(spread.at[:, 0:HALO], rim_in.at[1], 12, to_left),
        send(spread.at[:, HALO + COLS : EXT], rim_in.at[0], 13, to_right),
    ]
    for copy in edges:
        copy.wait()
    under = jnp.where(slab > 0, mis_in[0], 0.0)
    over = jnp.where(slab < slabs - 1, mis_in[1], 0.0)
    gradient = mid + (cen[...] * misfit + vertical(misfit, under, over) + spread[:, HALO : HALO + COLS])
    for copy in rims:
        copy.wait()
    gradient = gradient + jnp.concatenate([rim_in[0], rim_in[1]], axis=1)
    gradient_ref[...] = gradient

    for i in range(M):
        for name, value in (("sg", steps[i]), ("yg", grads[i])):
            slot[name, i] = len(slot)
            at = slot[name, i]
            prods[at : at + 1, :] = lane_sums(value.astype(F32) * gradient)

    def reduced(value, buf, me, peers, sends, recvs):
        count = len(peers) + 1
        buf[me] = value
        copies = []
        for d, peer in enumerate(peers):
            copy = pltpu.make_async_remote_copy(
                src_ref=buf.at[me],
                dst_ref=buf.at[me],
                send_sem=sends.at[d],
                recv_sem=recvs.at[d],
                device_id=peer,
                device_id_type=pl.DeviceIdType.MESH,
            )
            copy.start()
            copies.append(copy)
        for copy in copies:
            copy.wait()
        total = buf[0]
        for i in range(1, count):
            total = total + buf[i]
        return total

    total = jnp.sum(prods[...].T, axis=0, keepdims=True)
    total = reduced(total, red_lev, slab, lev_peers, lev_send, lev_recv)
    total = reduced(total, red_y, row_y, y_peers, y_send, y_recv)
    total = reduced(total, red_z, row_z, z_peers, z_send, z_recv)

    spreaded = jnp.broadcast_to(total, (128, 128)).T
    of = {name: spreaded[at : at + 1, :] for name, at in slot.items()}
    rho = [1.0 / of["sy", i, i] for i in range(M)]
    alpha = [None] * M
    for i in range(M - 1, -1, -1):
        value = of["sg", i]
        for j in range(i + 1, M):
            value = value - alpha[j] * of["sy", i, j]
        alpha[i] = rho[i] * value
    gamma = of["sy", M - 1, M - 1] / of["yy", M - 1, M - 1]
    keep = []
    for i in range(M):
        value = of["yg", i]
        for j in range(M):
            value = value - alpha[j] * of["yy", min(i, j), max(i, j)]
        value = gamma * value
        for j in range(i):
            value = value + keep[j] * of["sy", j, i]
        keep.append(alpha[i] - rho[i] * value)

    def wide(value):
        return jnp.concatenate([value] * (COLS // 128), axis=1)

    result = wide(-gamma) * gradient_ref[...]
    for i in range(M):
        result = result + wide(gamma * alpha[i]) * grads[i].astype(F32)
        result = result - wide(keep[i]) * steps[i].astype(F32)
    direction_ref[...] = result


def per_device(tiles, slabs, *args):
    (dep, off, wgt, cnt, inc, cen, vc, nbr, cpl, steps, grads) = args
    cnt = cnt.reshape(1, COLS)
    vmem = pltpu.VMEM
    sems = pltpu.SemaphoreType.DMA
    nz = tiles // NY
    shape = jax.ShapeDtypeStruct((ROWS, COLS), F32)
    return pl.pallas_call(
        functools.partial(kernel, tiles, slabs),
        out_shape=(shape, shape),
        in_specs=[pl.BlockSpec(memory_space=pl.ANY)] * 11,
        out_specs=[pl.BlockSpec(memory_space=vmem)] * 2,
        scratch_shapes=[
            vmem((ROWS, FINE), F32),
            vmem((K, COLS), I32),
            vmem((K, COLS), F32),
            vmem((1, COLS), I32),
            vmem((ROWS, COLS), F32),
            vmem((ROWS, COLS), F32),
            vmem((4, COLS), I32),
            vmem((4, COLS), F32),
            vmem((M, ROWS, COLS), BF16),
            vmem((M, ROWS, COLS), BF16),
            vmem((SEG, 128), F32),
            vmem(((OWN + FOREIGN) * K * 128, 128), F32),
            vmem(((OWN + FOREIGN) * 128, 128), F32),
            vmem((OWN, K, 128), I32),
            vmem((OWN, K, 128), F32),
            vmem((OWN, K, 128), I32),
            vmem((FOREIGN, K, 128), I32),
            vmem((FOREIGN, K, 128), F32),
            vmem((FOREIGN, K, 128), I32),
            vmem((FOREIGN, K, 128), F32),
            vmem((FOREIGN, K, 128), I32),
            pltpu.SMEM((OWN, K, 128), I32),
            pltpu.SMEM((FOREIGN, K, 128), I32),
            vmem((ROWS, EXT), F32),
            vmem((2 * ROWS, EXT), BF16),
            vmem((2, COLS // WIDE, REACH, WIDE), BF16),
            vmem((2, COLS), F32),
            vmem((2, COLS), F32),
            vmem((1, COLS), F32),
            vmem((1, COLS), F32),
            vmem((2, ROWS, EDGE), F32),
            vmem((2, ROWS, EDGE), F32),
            vmem((ROWS, COLS), F32),
            vmem((2, 1, COLS), F32),
            vmem((2, 1, COLS), F32),
            vmem((ROWS, EXT), F32),
            vmem((2, ROWS, HALO), F32),
            vmem((128, 128), F32),
            vmem((slabs, 1, 128), F32),
            vmem((NY, 1, 128), F32),
            vmem((nz, 1, 128), F32),
            sems((13,)),
            sems((14,)),
            sems((14,)),
            sems((slabs,)),
            sems((slabs,)),
            sems((NY,)),
            sems((NY,)),
            sems((nz,)),
            sems((nz,)),
        ],
        compiler_params=pltpu.CompilerParams(
            collective_id=0, has_side_effects=True, vmem_limit_bytes=48 * 1024 * 1024
        ),
        cost_estimate=pl.CostEstimate(flops=1 << 28, bytes_accessed=1 << 22, transcendentals=0),
    )(dep, off, wgt, cnt, inc, cen, vc, nbr, cpl, steps, grads)


def solution(mesh):
    tiles, slabs = mesh.shape["cols"], mesh.shape["lev"]
    return jax.shard_map(
        functools.partial(per_device, tiles, slabs),
        mesh=mesh,
        in_specs=(
            P("lev", "cols"),
            P(None, "cols"),
            P(None, "cols"),
            P("cols"),
            P("lev", "cols"),
            P("lev", "cols"),
            P("lev", "cols"),
            P(None, "cols"),
            P(None, "cols"),
            P(None, "lev", "cols"),
            P(None, "lev", "cols"),
        ),
        out_specs=(P("lev", "cols"), P("lev", "cols")),
        check_vma=False,
    )
```

```python
import functools

import jax
import jax.numpy as jnp
from jax import lax
from jax.experimental import pallas as pl
from jax.experimental.pallas import tpu as pltpu
from jax.sharding import PartitionSpec as P

K = 8
M = 4
RATIO = 31
ROWS = 16
COLS = 1024
FINE = RATIO * COLS
SEG = 4096
HALO = 512
EXT = COLS + 2 * HALO
EDGE = 384
OWN = COLS // 128
FOREIGN = 5
EARLY = 3
WIDE = 256
REACH = WIDE + HALO
NY = 4
F32 = jnp.float32
I32 = jnp.int32
BF16 = jnp.bfloat16


def halves(value):
    high = value.astype(BF16)
    low = (value - high.astype(F32)).astype(BF16)
    return jnp.concatenate([high, low], axis=0)


def lane_sums(value):
    total = value[0:8] + value[8:16]
    parts = [total[:, 128 * i : 128 * i + 128] for i in range(COLS // 128)]
    while len(parts) > 1:
        parts = [parts[i] + parts[i + 1] for i in range(0, len(parts), 2)]
    return jnp.sum(parts[0], axis=0, keepdims=True)


def kernel(
    tiles,
    slabs,
    dep_hbm,
    off_hbm,
    wgt_hbm,
    cnt_hbm,
    inc_hbm,
    cen_hbm,
    vc_hbm,
    nbr_hbm,
    cpl_hbm,
    step_hbm,
    grad_hbm,
    gradient_ref,
    direction_ref,
    dep,
    off,
    wgt,
    cnt,
    cen,
    vc,
    nbr,
    cpl,
    steps,
    grads,
    fine,
    rows_a,
    rows_b,
    result,
    f_all,
    w_all,
    r_all,
    f_out,
    w_out,
    f_for,
    w_for,
    index,
    inc,
    parts,
    onehot,
    up_out,
    below,
    down_out,
    above,
    sum_out,
    sum_in,
    mis_out,
    mis_in,
    spread,
    rim_in,
    prods,
    red_lev,
    red_y,
    red_z,
    local_sem,
    send_sem,
    recv_sem,
    lev_send,
    lev_recv,
    y_send,
    y_recv,
    z_send,
    z_recv,
):
    tile = lax.axis_index("cols")
    slab = lax.axis_index("lev")
    nz = tiles // NY
    row_z = tile // NY
    row_y = lax.rem(tile, NY)
    left = lax.rem(tile + tiles - 1, tiles)
    right = lax.rem(tile + 1, tiles)
    lower = lax.rem(slab + slabs - 1, slabs)
    upper = lax.rem(slab + 1, slabs)

    def spot(column, level):
        return {"cols": column, "lev": level}

    lev_peers = [spot(tile, lax.rem(slab + d, slabs)) for d in range(1, slabs)]
    y_peers = [spot(row_z * NY + lax.rem(row_y + d, NY), slab) for d in range(1, NY)]
    z_peers = [spot(lax.rem(row_z + d, nz) * NY + row_y, slab) for d in range(1, nz)]

    def remote(src, dst, i, target):
        return pltpu.make_async_remote_copy(
            src_ref=src,
            dst_ref=dst,
            send_sem=send_sem.at[i],
            recv_sem=recv_sem.at[i],
            device_id=target,
            device_id_type=pl.DeviceIdType.MESH,
        )

    def send(src, dst, i, target):
        copy = remote(src, dst, i, target)
        copy.start()
        return copy

    loads = []
    for i, (src, dst) in enumerate(
        [
            (off_hbm, off),
            (wgt_hbm, wgt),
            (cnt_hbm, cnt),
            (inc_hbm, inc.at[:, HALO : HALO + COLS]),
            (vc_hbm, vc),
            (dep_hbm, dep),
            (nbr_hbm, nbr),
            (cpl_hbm, cpl),
            (cen_hbm, cen),
            (step_hbm, steps),
            (grad_hbm, grads),
        ]
    ):
        copy = pltpu.make_async_copy(src, dst, local_sem.at[i])
        copy.start()
        loads.append(copy)

    barrier = pltpu.get_barrier_semaphore()
    greeted = lev_peers + y_peers + z_peers + [spot(left, slab), spot(right, slab)]
    for peer in greeted:
        pl.semaphore_signal(barrier, inc=1, device_id=peer, device_id_type=pl.DeviceIdType.MESH)

    for i in range(5):
        loads[i].wait()

    half = EDGE // 128
    lane = lax.broadcasted_iota(I32, (8, 128), 1)
    entry = lax.broadcasted_iota(I32, (8, 128), 0)
    for b in range(OWN):
        cut = slice(128 * b, 128 * b + 128)
        f = RATIO * (128 * b + lane) + off[:, cut]
        w = jnp.where(entry < cnt[:, cut], wgt[:, cut], 0.0)
        here = (f >= 0) & (f < FINE)
        fo = jnp.where(here, f, 0)
        f_all[b] = fo
        r_all[b * K : (b + 1) * K, :] = fo & (SEG - 1)
        w_all[b] = jnp.where(here, w, 0.0)
        if b < half:
            f_out[b] = jnp.where(f < 0, f + FINE, 0)
            w_out[b] = jnp.where(f < 0, w, 0.0)
        if b >= OWN - half:
            at = b - OWN + 2 * half
            f_out[at] = jnp.where(f >= FINE, f - FINE, 0)
            w_out[at] = jnp.where(f >= FINE, w, 0.0)
    own_index = pltpu.make_async_copy(r_all.at[0 : OWN * K], index.at[0 : OWN * K], local_sem.at[11])
    own_index.start()
    up_out[0:1, :] = inc[ROWS - 1 : ROWS, HALO : HALO + COLS]
    up_out[1:2, :] = vc[ROWS - 1 : ROWS, :]
    down_out[...] = inc[0:1, HALO : HALO + COLS]

    pl.semaphore_wait(barrier, len(greeted))

    to_left, to_right = spot(left, slab), spot(right, slab)
    to_lower, to_upper = spot(tile, lower), spot(tile, upper)
    lists = [
        send(f_out.at[0:half], f_for.at[0:half], 0, to_left),
        send(w_out.at[0:half], w_for.at[0:half], 1, to_left),
        send(f_out.at[half : 2 * half], f_for.at[half : 2 * half], 2, to_right),
        send(w_out.at[half : 2 * half], w_for.at[half : 2 * half], 3, to_right),
    ]
    halos = [
        send(inc.at[:, HALO : 2 * HALO], inc.at[:, HALO + COLS : EXT], 4, to_left),
        send(inc.at[:, COLS : COLS + HALO], inc.at[:, 0:HALO], 5, to_right),
        send(up_out, below, 6, to_upper),
        send(down_out, above, 7, to_lower),
    ]

    loads[5].wait()
    last = FINE // SEG
    tail = FINE - last * SEG
    for b in range(SEG // 128):
        pieces = [dep[:, SEG * g + 128 * b : SEG * g + 128 * b + 128] for g in range(last)]
        if 128 * b < tail:
            pieces.append(dep[:, SEG * last + 128 * b : SEG * last + 128 * b + 128])
        else:
            pieces.append(jnp.zeros((ROWS, 128), F32))
        fine[128 * b : 128 * b + 128, :] = jnp.concatenate(pieces, axis=0).T

    def gather(b, rows, lanes):
        for u in lanes:
            for k in range(K):
                rows[k * 128 + u : k * 128 + u + 1, :] = fine[pl.ds(index[b * K + k, u], 1), :]

    def weighed(b, rows):
        segment = f_all[b] // SEG
        weights = w_all[b]
        chosen = [jnp.where(segment == g, weights, 0.0) for g in range(8)]
        total = jnp.zeros((ROWS, 128), F32)
        for k in range(K):
            flat = rows[128 * k : 128 * k + 128, :].T
            for g in range(8):
                total = total + chosen[g][k : k + 1, :] * flat[ROWS * g : ROWS * g + ROWS]
        return total

    def block_of(i):
        return jnp.where(i < EARLY, 2 * i, jnp.where(i < EARLY + 2, OWN + 2 * (i - EARLY), 2 * (i - 2)))

    for_index = pltpu.make_async_copy(
        r_all.at[OWN * K : (OWN + FOREIGN) * K], index.at[OWN * K : (OWN + FOREIGN) * K], local_sem.at[12]
    )
    edge = OWN + FOREIGN - 1

    def pair(i, carry):
        @pl.when(i == EARLY - 1)
        def _():
            for copy in lists:
                copy.wait()
            for at, b in enumerate((0, 1, 4, 5)):
                f_all[OWN + at] = f_for[b]
                w_all[OWN + at] = w_for[b]
                r_all[(OWN + at) * K : (OWN + at + 1) * K, :] = f_for[b] & (SEG - 1)
            f_all[edge] = jnp.where(lane < 64, f_for[2], f_for[3])
            w_all[edge] = jnp.where(lane < 64, w_for[2], w_for[3])
            r_all[edge * K : (edge + 1) * K, :] = f_all[edge] & (SEG - 1)
            for_index.start()

        @pl.when(i == EARLY)
        def _():
            for_index.wait()

        @pl.when(i == EARLY + 2)
        def _():
            gather(edge, rows_a, [*range(16), *range(112, 128)])
            far = weighed(edge - 1, rows_b)
            rest = weighed(edge, rows_a)
            at = lax.broadcasted_iota(I32, (ROWS, 128), 1)
            sum_out[0, :, 0:128] = result[OWN]
            sum_out[0, :, 128:256] = result[OWN + 1]
            sum_out[0, :, 256:384] = jnp.where(at < 64, rest, 0.0)
            sum_out[1, :, 0:128] = jnp.where(at < 64, 0.0, rest)
            sum_out[1, :, 128:256] = result[OWN + 2]
            sum_out[1, :, 256:384] = far
            for copy in sums:
                copy.start()

        b = block_of(i)
        before = jnp.where(i == 0, edge + 1, block_of(i - 1) + 1)
        gather(b, rows_a, range(128))
        result[before] = weighed(before, rows_b)
        gather(b + 1, rows_b, range(128))
        result[b] = weighed(b, rows_a)
        return carry

    sums = [
        remote(sum_out.at[0], sum_in.at[0], 8, to_right),
        remote(sum_out.at[1], sum_in.at[1], 9, to_left),
    ]
    own_index.wait()
    f_all[edge + 1] = jnp.zeros((K, 128), I32)
    w_all[edge + 1] = jnp.zeros((K, 128), F32)
    rows_b[...] = jnp.zeros((K * 128, 128), F32)
    lax.fori_loop(0, (OWN + FOREIGN - 1) // 2, pair, 0)
    result[OWN - 1] = weighed(OWN - 1, rows_b)

    for i in range(6, 9):
        loads[i].wait()
    spots = (nbr[...] - tile * COLS + HALO) & (tiles * COLS - 1)
    for side in range(2):
        for b in range(COLS // WIDE):
            where = spots[2 + side : 3 + side, WIDE * b : WIDE * b + WIDE] - (WIDE * b + HALO * side)
            hit = lax.broadcasted_iota(I32, (REACH, WIDE), 0) == where
            onehot[side, b] = jnp.where(hit, 1.0, 0.0).astype(BF16)

    for copy in halos:
        copy.wait()
    parts[...] = halves(inc[...])
    mid = inc[:, HALO : HALO + COLS]
    row = lax.broadcasted_iota(I32, (ROWS, COLS), 0)
    couplings = vc[...]
    below_row = jnp.where(slab > 0, below[0:1, :], 0.0)
    below_coupling = jnp.where(slab > 0, below[1:2, :], 0.0)
    above_row = jnp.where(slab < slabs - 1, above[...], 0.0)
    couplings_down = jnp.where(row == 0, below_coupling, pltpu.roll(couplings, 1, 0))

    def vertical(value, under, over):
        up = jnp.where(row == ROWS - 1, over, pltpu.roll(value, ROWS - 1, 0))
        down = jnp.where(row == 0, under, pltpu.roll(value, 1, 0))
        return couplings * up + couplings_down * down

    image = cen[...] * mid + vertical(mid, below_row, above_row)
    around = inc[:, HALO - 128 : HALO + COLS + 128]
    image = image + cpl[0:1, :] * pltpu.roll(around, 1, 1)[:, 128 : 128 + COLS]
    image = image + cpl[1:2, :] * pltpu.roll(around, COLS + 255, 1)[:, 128 : 128 + COLS]
    blocks = []
    for b in range(COLS // WIDE):
        total = None
        for side in range(2):
            start = WIDE * b + HALO * side
            got = jnp.dot(parts[:, start : start + REACH], onehot[side, b], preferred_element_type=F32)
            term = cpl[2 + side : 3 + side, WIDE * b : WIDE * b + WIDE] * (got[0:ROWS] + got[ROWS : 2 * ROWS])
            total = term if total is None else total + term
        blocks.append(total)
    image = image + jnp.concatenate(blocks, axis=1)

    for i in range(9, 11):
        loads[i].wait()
    prods[...] = jnp.zeros((128, 128), F32)
    slot = {}
    for i in range(M):
        y_i = grads[i].astype(F32)
        s_i = steps[i].astype(F32)
        for j in range(i, M):
            y_j = grads[j].astype(F32)
            for name, value in (("sy", s_i), ("yy", y_i)):
                slot[name, i, j] = len(slot)
                at = slot[name, i, j]
                prods[at : at + 1, :] = lane_sums(value * y_j)

    for copy in sums:
        copy.wait()
    blank = jnp.zeros((ROWS, COLS - 2 * EDGE), F32)
    restricted = jnp.concatenate([result[b] for b in range(OWN)], axis=1)
    restricted = restricted + jnp.concatenate([sum_in[0], blank, sum_in[1]], axis=1)
    misfit = image - restricted
    mis_out[0] = misfit[ROWS - 1 : ROWS, :]
    mis_out[1] = misfit[0:1, :]
    edges = [
        send(mis_out.at[0], mis_in.at[0], 10, to_upper),
        send(mis_out.at[1], mis_in.at[1], 11, to_lower),
    ]

    spread[...] = jnp.zeros((ROWS, EXT), F32)
    blank = jnp.zeros((ROWS, 128), F32)
    back = jnp.concatenate([blank, cpl[0:1, :] * misfit, blank], axis=1)
    forth = jnp.concatenate([blank, cpl[1:2, :] * misfit, blank], axis=1)
    spread[:, HALO - 128 : HALO + COLS + 128] = pltpu.roll(back, COLS + 255, 1) + pltpu.roll(forth, 1, 1)
    for b in range(COLS // WIDE):
        for side in range(2):
            start = WIDE * b + HALO * side
            carried = halves(cpl[2 + side : 3 + side, WIDE * b : WIDE * b + WIDE] * misfit[:, WIDE * b : WIDE * b + WIDE])
            out = lax.dot_general(
                carried, onehot[side, b], (((1,), (1,)), ((), ())), preferred_element_type=F32
            )
            spread[:, start : start + REACH] = spread[:, start : start + REACH] + (out[0:ROWS] + out[ROWS : 2 * ROWS])
    rims = [
        send(spread.at[:, 0:HALO], rim_in.at[1], 12, to_left),
        send(spread.at[:, HALO + COLS : EXT], rim_in.at[0], 13, to_right),
    ]
    for copy in edges:
        copy.wait()
    under = jnp.where(slab > 0, mis_in[0], 0.0)
    over = jnp.where(slab < slabs - 1, mis_in[1], 0.0)
    gradient = mid + (cen[...] * misfit + vertical(misfit, under, over) + spread[:, HALO : HALO + COLS])
    for copy in rims:
        copy.wait()
    gradient = gradient + jnp.concatenate([rim_in[0], rim_in[1]], axis=1)
    gradient_ref[...] = gradient

    for i in range(M):
        for name, value in (("sg", steps[i]), ("yg", grads[i])):
            slot[name, i] = len(slot)
            at = slot[name, i]
            prods[at : at + 1, :] = lane_sums(value.astype(F32) * gradient)

    def reduced(value, buf, me, peers, sends, recvs):
        count = len(peers) + 1
        buf[me] = value
        copies = []
        for d, peer in enumerate(peers):
            copy = pltpu.make_async_remote_copy(
                src_ref=buf.at[me],
                dst_ref=buf.at[me],
                send_sem=sends.at[d],
                recv_sem=recvs.at[d],
                device_id=peer,
                device_id_type=pl.DeviceIdType.MESH,
            )
            copy.start()
            copies.append(copy)
        for copy in copies:
            copy.wait()
        total = buf[0]
        for i in range(1, count):
            total = total + buf[i]
        return total

    total = jnp.sum(prods[...].T, axis=0, keepdims=True)
    total = reduced(total, red_lev, slab, lev_peers, lev_send, lev_recv)
    total = reduced(total, red_y, row_y, y_peers, y_send, y_recv)
    total = reduced(total, red_z, row_z, z_peers, z_send, z_recv)

    spreaded = jnp.broadcast_to(total, (128, 128)).T
    of = {name: spreaded[at : at + 1, :] for name, at in slot.items()}
    rho = [1.0 / of["sy", i, i] for i in range(M)]
    alpha = [None] * M
    for i in range(M - 1, -1, -1):
        value = of["sg", i]
        for j in range(i + 1, M):
            value = value - alpha[j] * of["sy", i, j]
        alpha[i] = rho[i] * value
    gamma = of["sy", M - 1, M - 1] / of["yy", M - 1, M - 1]
    keep = []
    for i in range(M):
        value = of["yg", i]
        for j in range(M):
            value = value - alpha[j] * of["yy", min(i, j), max(i, j)]
        value = gamma * value
        for j in range(i):
            value = value + keep[j] * of["sy", j, i]
        keep.append(alpha[i] - rho[i] * value)

    def wide(value):
        return jnp.concatenate([value] * (COLS // 128), axis=1)

    result = wide(-gamma) * gradient_ref[...]
    for i in range(M):
        result = result + wide(gamma * alpha[i]) * grads[i].astype(F32)
        result = result - wide(keep[i]) * steps[i].astype(F32)
    direction_ref[...] = result


def per_device(tiles, slabs, *args):
    (dep, off, wgt, cnt, inc, cen, vc, nbr, cpl, steps, grads) = args
    cnt = cnt.reshape(1, COLS)
    vmem = pltpu.VMEM
    sems = pltpu.SemaphoreType.DMA
    nz = tiles // NY
    shape = jax.ShapeDtypeStruct((ROWS, COLS), F32)
    return pl.pallas_call(
        functools.partial(kernel, tiles, slabs),
        out_shape=(shape, shape),
        in_specs=[pl.BlockSpec(memory_space=pltpu.HBM)] * 11,
        out_specs=[pl.BlockSpec(memory_space=vmem)] * 2,
        scratch_shapes=[
            vmem((ROWS, FINE), F32),
            vmem((K, COLS), I32),
            vmem((K, COLS), F32),
            vmem((1, COLS), I32),
            vmem((ROWS, COLS), F32),
            vmem((ROWS, COLS), F32),
            vmem((4, COLS), I32),
            vmem((4, COLS), F32),
            vmem((M, ROWS, COLS), BF16),
            vmem((M, ROWS, COLS), BF16),
            vmem((SEG, 128), F32),
            vmem((K * 128, 128), F32),
            vmem((K * 128, 128), F32),
            vmem((OWN + FOREIGN + 1, ROWS, 128), F32),
            vmem((OWN + FOREIGN + 1, K, 128), I32),
            vmem((OWN + FOREIGN + 1, K, 128), F32),
            vmem(((OWN + FOREIGN) * K, 128), I32),
            vmem((2 * EDGE // 128, K, 128), I32),
            vmem((2 * EDGE // 128, K, 128), F32),
            vmem((2 * EDGE // 128, K, 128), I32),
            vmem((2 * EDGE // 128, K, 128), F32),
            pltpu.SMEM(((OWN + FOREIGN) * K, 128), I32),
            vmem((ROWS, EXT), F32),
            vmem((2 * ROWS, EXT), BF16),
            vmem((2, COLS // WIDE, REACH, WIDE), BF16),
            vmem((2, COLS), F32),
            vmem((2, COLS), F32),
            vmem((1, COLS), F32),
            vmem((1, COLS), F32),
            vmem((2, ROWS, EDGE), F32),
            vmem((2, ROWS, EDGE), F32),
            vmem((2, 1, COLS), F32),
            vmem((2, 1, COLS), F32),
            vmem((ROWS, EXT), F32),
            vmem((2, ROWS, HALO), F32),
            vmem((128, 128), F32),
            vmem((slabs, 1, 128), F32),
            vmem((NY, 1, 128), F32),
            vmem((nz, 1, 128), F32),
            sems((13,)),
            sems((14,)),
            sems((14,)),
            sems((slabs,)),
            sems((slabs,)),
            sems((NY,)),
            sems((NY,)),
            sems((nz,)),
            sems((nz,)),
        ],
        compiler_params=pltpu.CompilerParams(
            collective_id=0, has_side_effects=True, vmem_limit_bytes=60 * 1024 * 1024
        ),
        cost_estimate=pl.CostEstimate(flops=1 << 28, bytes_accessed=1 << 22, transcendentals=0),
    )(dep, off, wgt, cnt, inc, cen, vc, nbr, cpl, steps, grads)


def solution(mesh):
    tiles, slabs = mesh.shape["cols"], mesh.shape["lev"]
    return jax.shard_map(
        functools.partial(per_device, tiles, slabs),
        mesh=mesh,
        in_specs=(
            P("lev", "cols"),
            P(None, "cols"),
            P(None, "cols"),
            P("cols"),
            P("lev", "cols"),
            P("lev", "cols"),
            P("lev", "cols"),
            P(None, "cols"),
            P(None, "cols"),
            P(None, "lev", "cols"),
            P(None, "lev", "cols"),
        ),
        out_specs=(P("lev", "cols"), P("lev", "cols")),
        check_vma=False,
    )
```

```python
import functools

import jax
import jax.numpy as jnp
from jax import lax
from jax.experimental import pallas as pl
from jax.experimental.pallas import tpu as pltpu
from jax.sharding import PartitionSpec as P

K = 8
M = 4
RATIO = 31
ROWS = 16
COLS = 1024
FINE = RATIO * COLS
SEG = 4096
HALO = 512
EXT = COLS + 2 * HALO
EDGE = 384
OWN = COLS // 128
FOREIGN = 5
EARLY = 3
WIDE = 256
REACH = WIDE + HALO
NY = 4
F32 = jnp.float32
I32 = jnp.int32
BF16 = jnp.bfloat16


def halves(value):
    high = value.astype(BF16)
    low = (value - high.astype(F32)).astype(BF16)
    return jnp.concatenate([high, low], axis=0)


def lane_blocks(value):
    parts = [value[:, 128 * i : 128 * i + 128] for i in range(value.shape[1] // 128)]
    while len(parts) > 1:
        parts = [parts[i] + parts[i + 1] for i in range(0, len(parts), 2)]
    return parts[0]


def lane_sums(value):
    return jnp.sum(lane_blocks(value[0:8] + value[8:16]), axis=0, keepdims=True)


def kernel(
    tiles,
    slabs,
    dep_hbm,
    off_hbm,
    wgt_hbm,
    cnt_hbm,
    inc_hbm,
    cen_hbm,
    vc_hbm,
    nbr_hbm,
    cpl_hbm,
    step_hbm,
    grad_hbm,
    gradient_hbm,
    direction_hbm,
    dep,
    off,
    wgt,
    cnt,
    cen,
    vc,
    nbr,
    cpl,
    steps,
    grads,
    fine,
    rows_a,
    rows_b,
    result,
    f_all,
    w_all,
    r_all,
    f_out,
    w_out,
    f_for,
    w_for,
    slots,
    inc,
    parts,
    onehot,
    up_out,
    below,
    down_out,
    above,
    sum_out,
    sum_in,
    mis_out,
    mis_in,
    spread,
    rim_in,
    pairs,
    pair_up,
    pair_below,
    pair_down,
    pair_above,
    gradient,
    direction,
    prods,
    red_plane,
    red_z,
    local_sem,
    slot_sem,
    send_sem,
    recv_sem,
    plane_send,
    plane_recv,
    z_send,
    z_recv,
):
    tile = lax.axis_index("cols")
    slab = lax.axis_index("lev")
    nz = tiles // NY
    row_z = tile // NY
    row_y = lax.rem(tile, NY)
    left = lax.rem(tile + tiles - 1, tiles)
    right = lax.rem(tile + 1, tiles)
    lower = lax.rem(slab + slabs - 1, slabs)
    upper = lax.rem(slab + 1, slabs)

    def spot(column, level):
        return {"cols": column, "lev": level}

    def around(count):
        return sorted(range(1, count), key=lambda d: -min(d, count - d))

    plane_peers = [
        spot(row_z * NY + lax.rem(row_y + e, NY), lax.rem(slab + d, slabs))
        for e in around(NY) + [0]
        for d in around(slabs) + [0]
        if d or e
    ]
    z_peers = [spot(lax.rem(row_z + d, nz) * NY + row_y, slab) for d in around(nz)]

    def remote(src, dst, i, target):
        return pltpu.make_async_remote_copy(
            src_ref=src,
            dst_ref=dst,
            send_sem=send_sem.at[i],
            recv_sem=recv_sem.at[i],
            device_id=target,
            device_id_type=pl.DeviceIdType.MESH,
        )

    def send(src, dst, i, target):
        copy = remote(src, dst, i, target)
        copy.start()
        return copy

    loads = []
    for i, (src, dst) in enumerate(
        [
            (off_hbm, off),
            (wgt_hbm, wgt),
            (cnt_hbm, cnt),
            (inc_hbm, inc.at[:, HALO : HALO + COLS]),
            (vc_hbm, vc),
            (dep_hbm, dep),
            (nbr_hbm, nbr),
            (cpl_hbm, cpl),
            (cen_hbm, cen),
            (step_hbm, steps),
            (grad_hbm, grads),
        ]
    ):
        copy = pltpu.make_async_copy(src, dst, local_sem.at[i])
        copy.start()
        loads.append(copy)

    barrier = pltpu.get_barrier_semaphore()
    greeted = plane_peers + z_peers + [spot(left, slab), spot(right, slab)]
    for peer in greeted:
        pl.semaphore_signal(barrier, inc=1, device_id=peer, device_id_type=pl.DeviceIdType.MESH)

    for i in range(5):
        loads[i].wait()

    half = EDGE // 128
    lane = lax.broadcasted_iota(I32, (8, 128), 1)
    entry = lax.broadcasted_iota(I32, (8, 128), 0)
    for b in range(OWN):
        cut = slice(128 * b, 128 * b + 128)
        f = RATIO * (128 * b + lane) + off[:, cut]
        w = jnp.where(entry < cnt[:, cut], wgt[:, cut], 0.0)
        here = (f >= 0) & (f < FINE)
        fo = jnp.where(here, f, 0)
        f_all[b] = fo
        r_all[b] = fo & (SEG - 1)
        w_all[b] = jnp.where(here, w, 0.0)
        if b < half:
            f_out[b] = jnp.where(f < 0, f + FINE, 0)
            w_out[b] = jnp.where(f < 0, w, 0.0)
        if b >= OWN - half:
            at = b - OWN + 2 * half
            f_out[at] = jnp.where(f >= FINE, f - FINE, 0)
            w_out[at] = jnp.where(f >= FINE, w, 0.0)

    def fetch(b, at):
        return pltpu.make_async_copy(r_all.at[b], slots.at[at], slot_sem.at[at])

    fetch(0, 0).start()
    fetch(1, 1).start()
    up_out[0:1, :] = inc[ROWS - 1 : ROWS, HALO : HALO + COLS]
    up_out[1:2, :] = vc[ROWS - 1 : ROWS, :]
    down_out[...] = inc[0:1, HALO : HALO + COLS]

    pl.semaphore_wait(barrier, len(greeted))

    to_left, to_right = spot(left, slab), spot(right, slab)
    to_lower, to_upper = spot(tile, lower), spot(tile, upper)
    lists = [
        send(f_out.at[0:half], f_for.at[0:half], 0, to_left),
        send(w_out.at[0:half], w_for.at[0:half], 1, to_left),
        send(f_out.at[half : 2 * half], f_for.at[half : 2 * half], 2, to_right),
        send(w_out.at[half : 2 * half], w_for.at[half : 2 * half], 3, to_right),
    ]
    halos = [
        send(inc.at[:, HALO : 2 * HALO], inc.at[:, HALO + COLS : EXT], 4, to_left),
        send(inc.at[:, COLS : COLS + HALO], inc.at[:, 0:HALO], 5, to_right),
        send(up_out, below, 6, to_upper),
        send(down_out, above, 7, to_lower),
    ]

    loads[5].wait()
    last = FINE // SEG
    tail = FINE - last * SEG
    for b in range(SEG // 128):
        pieces = [dep[:, SEG * g + 128 * b : SEG * g + 128 * b + 128] for g in range(last)]
        if 128 * b < tail:
            pieces.append(dep[:, SEG * last + 128 * b : SEG * last + 128 * b + 128])
        else:
            pieces.append(jnp.zeros((ROWS, 128), F32))
        fine[128 * b : 128 * b + 128, :] = jnp.concatenate(pieces, axis=0).T

    loads[9].wait()
    loads[10].wait()
    for i in range(M):
        for at, value in ((i, steps[i]), (M + i, grads[i])):
            field = value.astype(F32)
            pairs[at, :, HALO : HALO + COLS] = field
            pair_up[at : at + 1, :] = field[ROWS - 1 : ROWS]
            pair_down[at : at + 1, :] = field[0:1]
    halos += [
        send(pairs.at[:, :, HALO : 2 * HALO], pairs.at[:, :, HALO + COLS : EXT], 14, to_left),
        send(pairs.at[:, :, COLS : COLS + HALO], pairs.at[:, :, 0:HALO], 15, to_right),
        send(pair_up, pair_below, 16, to_upper),
        send(pair_down, pair_above, 17, to_lower),
    ]

    def gather(at, rows, lanes):
        for u in lanes:
            for k in range(K):
                rows[k * 128 + u : k * 128 + u + 1, :] = fine[pl.ds(slots[at, k, u], 1), :]

    def weighed(b, rows):
        segment = f_all[b] // SEG
        weights = w_all[b]
        chosen = [jnp.where(segment == g, weights, 0.0) for g in range(8)]
        total = jnp.zeros((ROWS, 128), F32)
        for k in range(K):
            flat = rows[128 * k : 128 * k + 128, :].T
            for g in range(8):
                total = total + chosen[g][k : k + 1, :] * flat[ROWS * g : ROWS * g + ROWS]
        return total

    def block_of(i):
        return jnp.where(i < EARLY, 2 * i, jnp.where(i < EARLY + 2, OWN + 2 * (i - EARLY), 2 * (i - 2)))

    edge = OWN + FOREIGN - 1
    turns = (OWN + FOREIGN - 1) // 2

    def pair(i, carry):
        @pl.when(i == EARLY - 1)
        def _():
            for copy in lists:
                copy.wait()
            for at, b in enumerate((0, 1, 4, 5)):
                f_all[OWN + at] = f_for[b]
                w_all[OWN + at] = w_for[b]
                r_all[OWN + at] = f_for[b] & (SEG - 1)
            f_all[edge] = jnp.where(lane < 64, f_for[2], f_for[3])
            w_all[edge] = jnp.where(lane < 64, w_for[2], w_for[3])
            r_all[edge] = f_all[edge] & (SEG - 1)
            fetch(edge, 2).start()

        @pl.when(i == EARLY + 2)
        def _():
            fetch(edge, 2).wait()
            gather(2, rows_a, [*range(16), *range(112, 128)])
            far = weighed(edge - 1, rows_b)
            rest = weighed(edge, rows_a)
            at = lax.broadcasted_iota(I32, (ROWS, 128), 1)
            sum_out[0, :, 0:128] = result[OWN]
            sum_out[0, :, 128:256] = result[OWN + 1]
            sum_out[0, :, 256:384] = jnp.where(at < 64, rest, 0.0)
            sum_out[1, :, 0:128] = jnp.where(at < 64, 0.0, rest)
            sum_out[1, :, 128:256] = result[OWN + 2]
            sum_out[1, :, 256:384] = far
            for copy in sums:
                copy.start()

        b = block_of(i)
        before = jnp.where(i == 0, edge + 1, block_of(i - 1) + 1)
        later = jnp.where(i < turns - 1, block_of(i + 1), 0)
        fetch(b, 0).wait()
        gather(0, rows_a, range(128))
        fetch(later, 0).start()
        result[before] = weighed(before, rows_b)
        fetch(b + 1, 1).wait()
        gather(1, rows_b, range(128))
        fetch(later + 1, 1).start()
        result[b] = weighed(b, rows_a)
        return carry

    sums = [
        remote(sum_out.at[0], sum_in.at[0], 8, to_right),
        remote(sum_out.at[1], sum_in.at[1], 9, to_left),
    ]
    f_all[edge + 1] = jnp.zeros((K, 128), I32)
    w_all[edge + 1] = jnp.zeros((K, 128), F32)
    rows_b[...] = jnp.zeros((K * 128, 128), F32)
    lax.fori_loop(0, turns, pair, 0)
    fetch(0, 0).wait()
    fetch(1, 1).wait()
    result[OWN - 1] = weighed(OWN - 1, rows_b)

    for i in range(6, 9):
        loads[i].wait()
    spots = (nbr[...] - tile * COLS + HALO) & (tiles * COLS - 1)
    for side in range(2):
        for b in range(COLS // WIDE):
            where = spots[2 + side : 3 + side, WIDE * b : WIDE * b + WIDE] - (WIDE * b + HALO * side)
            hit = lax.broadcasted_iota(I32, (REACH, WIDE), 0) == where
            onehot[side, b] = jnp.where(hit, 1.0, 0.0).astype(BF16)

    for copy in halos:
        copy.wait()
    parts[...] = halves(inc[...])
    mid = inc[:, HALO : HALO + COLS]
    row = lax.broadcasted_iota(I32, (ROWS, COLS), 0)
    couplings = vc[...]
    below_row = jnp.where(slab > 0, below[0:1, :], 0.0)
    below_coupling = jnp.where(slab > 0, below[1:2, :], 0.0)
    above_row = jnp.where(slab < slabs - 1, above[...], 0.0)
    couplings_down = jnp.where(row == 0, below_coupling, pltpu.roll(couplings, 1, 0))

    def vertical(value, under, over):
        up = jnp.where(row == ROWS - 1, over, pltpu.roll(value, ROWS - 1, 0))
        down = jnp.where(row == 0, under, pltpu.roll(value, 1, 0))
        return couplings * up + couplings_down * down

    image = cen[...] * mid + vertical(mid, below_row, above_row)
    near = inc[:, HALO - 128 : HALO + COLS + 128]
    image = image + cpl[0:1, :] * pltpu.roll(near, 1, 1)[:, 128 : 128 + COLS]
    image = image + cpl[1:2, :] * pltpu.roll(near, COLS + 255, 1)[:, 128 : 128 + COLS]
    blocks = []
    for b in range(COLS // WIDE):
        total = None
        for side in range(2):
            start = WIDE * b + HALO * side
            got = jnp.dot(parts[:, start : start + REACH], onehot[side, b], preferred_element_type=F32)
            term = cpl[2 + side : 3 + side, WIDE * b : WIDE * b + WIDE] * (got[0:ROWS] + got[ROWS : 2 * ROWS])
            total = term if total is None else total + term
        blocks.append(total)
    image = image + jnp.concatenate(blocks, axis=1)

    middle = slice(HALO, HALO + COLS)
    prods[...] = jnp.zeros((128, 128), F32)
    slot = {}
    for i in range(M):
        for j in range(i, M):
            for name, at in (("sy", i), ("yy", M + i)):
                here = slot[name, i, j] = len(slot)
                prods[here : here + 1, :] = lane_sums(pairs[at, :, middle] * pairs[M + j, :, middle])

    for copy in sums:
        copy.wait()
    blank = jnp.zeros((ROWS, COLS - 2 * EDGE), F32)
    restricted = jnp.concatenate([result[b] for b in range(OWN)], axis=1)
    restricted = restricted + jnp.concatenate([sum_in[0], blank, sum_in[1]], axis=1)
    misfit = image - restricted
    mis_out[0] = misfit[ROWS - 1 : ROWS, :]
    mis_out[1] = misfit[0:1, :]
    edges = [
        send(mis_out.at[0], mis_in.at[0], 10, to_upper),
        send(mis_out.at[1], mis_in.at[1], 11, to_lower),
    ]

    spread[...] = jnp.zeros((ROWS, EXT), F32)
    blank = jnp.zeros((ROWS, 128), F32)
    back = jnp.concatenate([blank, cpl[0:1, :] * misfit, blank], axis=1)
    forth = jnp.concatenate([blank, cpl[1:2, :] * misfit, blank], axis=1)
    spread[:, HALO - 128 : HALO + COLS + 128] = pltpu.roll(back, COLS + 255, 1) + pltpu.roll(forth, 1, 1)
    for b in range(COLS // WIDE):
        for side in range(2):
            start = WIDE * b + HALO * side
            carried = halves(cpl[2 + side : 3 + side, WIDE * b : WIDE * b + WIDE] * misfit[:, WIDE * b : WIDE * b + WIDE])
            out = lax.dot_general(
                carried, onehot[side, b], (((1,), (1,)), ((), ())), preferred_element_type=F32
            )
            spread[:, start : start + REACH] = spread[:, start : start + REACH] + (out[0:ROWS] + out[ROWS : 2 * ROWS])
    rims = [
        send(spread.at[:, 0:HALO], rim_in.at[:, COLS - HALO : COLS], 12, to_left),
        send(spread.at[:, HALO + COLS : EXT], rim_in.at[:, 0:HALO], 13, to_right),
    ]
    part = mid + (cen[...] * misfit + vertical(misfit, 0.0, 0.0) + spread[:, middle])

    late = 24
    to_below = below_coupling * misfit[0:1, :]
    to_above = jnp.where(slab < slabs - 1, couplings[ROWS - 1 : ROWS, :] * misfit[ROWS - 1 : ROWS, :], 0.0)
    beyond = lane_blocks(pair_below[...] * to_below + pair_above[...] * to_above)
    sides = []
    for at in range(2 * M):
        total = lane_blocks(pairs[at, :, 0:HALO] * spread[:, 0:HALO])
        total = total + lane_blocks(pairs[at, :, HALO + COLS : EXT] * spread[:, HALO + COLS : EXT])
        total = total + lane_blocks(pairs[at, :, middle] * part)
        sides.append(jnp.sum(total, axis=0, keepdims=True))
        slot["sg" if at < M else "yg", at % M] = late + at
    prods[late : late + 2 * M, :] = jnp.concatenate(sides, axis=0) + beyond

    def finish():
        for copy in edges:
            copy.wait()
        under = jnp.where(slab > 0, mis_in[0], 0.0)
        over = jnp.where(slab < slabs - 1, mis_in[1], 0.0)
        for copy in rims:
            copy.wait()
        whole = part + jnp.where(row == 0, couplings_down * under, 0.0)
        whole = whole + jnp.where(row == ROWS - 1, couplings * over, 0.0)
        gradient[...] = whole + rim_in[...]
        gradient_out.start()

    gradient_out = pltpu.make_async_copy(gradient, gradient_hbm, local_sem.at[11])
    direction_out = pltpu.make_async_copy(direction, direction_hbm, local_sem.at[12])

    def reduced(value, buf, me, peers, sends, recvs, beside=None):
        count = len(peers) + 1
        buf[me] = value
        copies = []
        for d, peer in enumerate(peers):
            copy = pltpu.make_async_remote_copy(
                src_ref=buf.at[me],
                dst_ref=buf.at[me],
                send_sem=sends.at[d],
                recv_sem=recvs.at[d],
                device_id=peer,
                device_id_type=pl.DeviceIdType.MESH,
            )
            copy.start()
            copies.append(copy)
        if beside is not None:
            beside()
        for copy in copies:
            copy.wait()
        total = buf[0]
        for i in range(1, count):
            total = total + buf[i]
        return total

    total = jnp.sum(prods[...].T, axis=0, keepdims=True)
    total = reduced(total, red_plane, row_y * slabs + slab, plane_peers, plane_send, plane_recv)
    total = reduced(total, red_z, row_z, z_peers, z_send, z_recv, finish)

    spreaded = jnp.broadcast_to(total, (128, 128)).T
    of = {name: spreaded[at : at + 1, :] for name, at in slot.items()}
    rho = [1.0 / of["sy", i, i] for i in range(M)]
    alpha = [None] * M
    for i in range(M - 1, -1, -1):
        value = of["sg", i]
        for j in range(i + 1, M):
            value = value - alpha[j] * of["sy", i, j]
        alpha[i] = rho[i] * value
    gamma = of["sy", M - 1, M - 1] / of["yy", M - 1, M - 1]
    keep = []
    for i in range(M):
        value = of["yg", i]
        for j in range(M):
            value = value - alpha[j] * of["yy", min(i, j), max(i, j)]
        value = gamma * value
        for j in range(i):
            value = value + keep[j] * of["sy", j, i]
        keep.append(alpha[i] - rho[i] * value)

    def wide(value):
        return jnp.concatenate([value] * (COLS // 128), axis=1)

    found = wide(-gamma) * gradient[...]
    for i in range(M):
        found = found + wide(gamma * alpha[i]) * pairs[M + i, :, middle]
        found = found - wide(keep[i]) * pairs[i, :, middle]
    direction[...] = found
    direction_out.start()
    gradient_out.wait()
    direction_out.wait()


def hand_over(first, second, first_out, second_out, staged, sem):
    pulls = [pltpu.make_async_copy(ref, staged.at[i], sem.at[i]) for i, ref in enumerate((first, second))]
    pushes = [
        pltpu.make_async_copy(staged.at[i], ref, sem.at[2 + i]) for i, ref in enumerate((first_out, second_out))
    ]
    for copy in pulls:
        copy.start()
    for pull, push in zip(pulls, pushes):
        pull.wait()
        push.start()
    for copy in pushes:
        copy.wait()


def per_device(tiles, slabs, *args):
    (dep, off, wgt, cnt, inc, cen, vc, nbr, cpl, steps, grads) = args
    cnt = cnt.reshape(1, COLS)
    vmem = pltpu.VMEM
    sems = pltpu.SemaphoreType.DMA
    nz = tiles // NY
    shape = jax.ShapeDtypeStruct((ROWS, COLS), F32)
    made = pl.pallas_call(
        functools.partial(kernel, tiles, slabs),
        out_shape=(shape, shape),
        in_specs=[pl.BlockSpec(memory_space=pltpu.HBM)] * 11,
        out_specs=[pl.BlockSpec(memory_space=pltpu.HBM)] * 2,
        scratch_shapes=[
            vmem((ROWS, FINE), F32),
            vmem((K, COLS), I32),
            vmem((K, COLS), F32),
            vmem((1, COLS), I32),
            vmem((ROWS, COLS), F32),
            vmem((ROWS, COLS), F32),
            vmem((4, COLS), I32),
            vmem((4, COLS), F32),
            vmem((M, ROWS, COLS), BF16),
            vmem((M, ROWS, COLS), BF16),
            vmem((SEG, 128), F32),
            vmem((K * 128, 128), F32),
            vmem((K * 128, 128), F32),
            vmem((OWN + FOREIGN + 1, ROWS, 128), F32),
            vmem((OWN + FOREIGN + 1, K, 128), I32),
            vmem((OWN + FOREIGN + 1, K, 128), F32),
            vmem((OWN + FOREIGN, K, 128), I32),
            vmem((2 * EDGE // 128, K, 128), I32),
            vmem((2 * EDGE // 128, K, 128), F32),
            vmem((2 * EDGE // 128, K, 128), I32),
            vmem((2 * EDGE // 128, K, 128), F32),
            pltpu.SMEM((3, K, 128), I32),
            vmem((ROWS, EXT), F32),
            vmem((2 * ROWS, EXT), BF16),
            vmem((2, COLS // WIDE, REACH, WIDE), BF16),
            vmem((2, COLS), F32),
            vmem((2, COLS), F32),
            vmem((1, COLS), F32),
            vmem((1, COLS), F32),
            vmem((2, ROWS, EDGE), F32),
            vmem((2, ROWS, EDGE), F32),
            vmem((2, 1, COLS), F32),
            vmem((2, 1, COLS), F32),
            vmem((ROWS, EXT), F32),
            vmem((ROWS, COLS), F32),
            vmem((2 * M, ROWS, EXT), F32),
            vmem((2 * M, COLS), F32),
            vmem((2 * M, COLS), F32),
            vmem((2 * M, COLS), F32),
            vmem((2 * M, COLS), F32),
            vmem((ROWS, COLS), F32),
            vmem((ROWS, COLS), F32),
            vmem((128, 128), F32),
            vmem((NY * slabs, 1, 128), F32),
            vmem((nz, 1, 128), F32),
            sems((13,)),
            sems((3,)),
            sems((18,)),
            sems((18,)),
            sems((NY * slabs,)),
            sems((NY * slabs,)),
            sems((nz,)),
            sems((nz,)),
        ],
        compiler_params=pltpu.CompilerParams(
            collective_id=0, has_side_effects=True, vmem_limit_bytes=60 * 1024 * 1024
        ),
        cost_estimate=pl.CostEstimate(flops=1 << 28, bytes_accessed=1 << 22, transcendentals=0),
    )(dep, off, wgt, cnt, inc, cen, vc, nbr, cpl, steps, grads)
    return pl.pallas_call(
        hand_over,
        out_shape=(shape, shape),
        in_specs=[pl.BlockSpec(memory_space=pltpu.HBM)] * 2,
        out_specs=[pl.BlockSpec(memory_space=pltpu.HBM)] * 2,
        scratch_shapes=[vmem((2, ROWS, COLS), F32), sems((4,))],
        compiler_params=pltpu.CompilerParams(vmem_limit_bytes=60 * 1024 * 1024),
    )(*made)


def solution(mesh):
    tiles, slabs = mesh.shape["cols"], mesh.shape["lev"]
    return jax.shard_map(
        functools.partial(per_device, tiles, slabs),
        mesh=mesh,
        in_specs=(
            P("lev", "cols"),
            P(None, "cols"),
            P(None, "cols"),
            P("cols"),
            P("lev", "cols"),
            P("lev", "cols"),
            P("lev", "cols"),
            P(None, "cols"),
            P(None, "cols"),
            P(None, "lev", "cols"),
            P(None, "lev", "cols"),
        ),
        out_specs=(P("lev", "cols"), P("lev", "cols")),
        check_vma=False,
    )
```

```python
import functools

import jax
import jax.numpy as jnp
from jax import lax
from jax.experimental import pallas as pl
from jax.experimental.pallas import tpu as pltpu
from jax.sharding import PartitionSpec as P

K = 8
M = 4
RATIO = 31
ROWS = 16
COLS = 1024
FINE = RATIO * COLS
SEG = 4096
HALO = 512
EXT = COLS + 2 * HALO
EDGE = 384
OWN = COLS // 128
FOREIGN = 5
EARLY = 2
WIDE = 256
REACH = WIDE + HALO
NY = 4
F32 = jnp.float32
I32 = jnp.int32
BF16 = jnp.bfloat16


def halves(value):
    high = value.astype(BF16)
    low = (value - high.astype(F32)).astype(BF16)
    return jnp.concatenate([high, low], axis=0)


def lane_blocks(value):
    parts = [value[:, 128 * i : 128 * i + 128] for i in range(value.shape[1] // 128)]
    while len(parts) > 1:
        parts = [parts[i] + parts[i + 1] for i in range(0, len(parts), 2)]
    return parts[0]


def lane_sums(value):
    return jnp.sum(lane_blocks(value[0:8] + value[8:16]), axis=0, keepdims=True)


def kernel(
    tiles,
    slabs,
    dep_hbm,
    off_hbm,
    wgt_hbm,
    cnt_hbm,
    inc_hbm,
    cen_hbm,
    vc_hbm,
    nbr_hbm,
    cpl_hbm,
    step_hbm,
    grad_hbm,
    gradient_hbm,
    direction_hbm,
    dep,
    off,
    wgt,
    cnt,
    cen,
    vc,
    nbr,
    cpl,
    steps,
    grads,
    fine,
    rows_a,
    rows_b,
    result,
    f_all,
    w_all,
    r_all,
    f_out,
    w_out,
    f_for,
    w_for,
    slots,
    inc,
    parts,
    up_out,
    below,
    down_out,
    above,
    sum_out,
    sum_in,
    mis_out,
    mis_in,
    spread,
    rim_in,
    pairs,
    pair_up,
    pair_below,
    pair_down,
    pair_above,
    gradient,
    direction,
    prods,
    red_plane,
    red_z,
    local_sem,
    dep_sem,
    slot_sem,
    send_sem,
    recv_sem,
    plane_send,
    plane_recv,
    z_send,
    z_recv,
):
    tile = lax.axis_index("cols")
    slab = lax.axis_index("lev")
    nz = tiles // NY
    row_z = tile // NY
    row_y = lax.rem(tile, NY)
    left = lax.rem(tile + tiles - 1, tiles)
    right = lax.rem(tile + 1, tiles)
    lower = lax.rem(slab + slabs - 1, slabs)
    upper = lax.rem(slab + 1, slabs)

    def spot(column, level):
        return {"cols": column, "lev": level}

    def around(count):
        return sorted(range(1, count), key=lambda d: -min(d, count - d))

    plane_peers = [
        spot(row_z * NY + lax.rem(row_y + e, NY), lax.rem(slab + d, slabs))
        for e in around(NY) + [0]
        for d in around(slabs) + [0]
        if d or e
    ]
    z_peers = [spot(lax.rem(row_z + d, nz) * NY + row_y, slab) for d in around(nz)]

    def remote(src, dst, i, target):
        return pltpu.make_async_remote_copy(
            src_ref=src,
            dst_ref=dst,
            send_sem=send_sem.at[i],
            recv_sem=recv_sem.at[i],
            device_id=target,
            device_id_type=pl.DeviceIdType.MESH,
        )

    def send(src, dst, i, target):
        copy = remote(src, dst, i, target)
        copy.start()
        return copy

    loads, cuts = [], []
    for i, (src, dst) in enumerate(
        [
            (off_hbm, off),
            (wgt_hbm, wgt),
            (cnt_hbm, cnt),
            (inc_hbm, inc.at[:, HALO : HALO + COLS]),
            (vc_hbm, vc),
            (nbr_hbm, nbr),
            (cpl_hbm, cpl),
            (cen_hbm, cen),
            (step_hbm, steps),
            (grad_hbm, grads),
        ]
    ):
        copy = pltpu.make_async_copy(src, dst, local_sem.at[i])
        copy.start()
        loads.append(copy)
        if i == 4:
            for g in range(8):
                part = slice(SEG * g, min(SEG * g + SEG, FINE))
                copy = pltpu.make_async_copy(dep_hbm.at[:, part], dep.at[:, part], dep_sem.at[g])
                copy.start()
                cuts.append(copy)

    barrier = pltpu.get_barrier_semaphore()
    greeted = plane_peers + z_peers + [spot(left, slab), spot(right, slab)]
    for peer in greeted:
        pl.semaphore_signal(barrier, inc=1, device_id=peer, device_id_type=pl.DeviceIdType.MESH)

    for i in range(5):
        loads[i].wait()

    half = EDGE // 128
    lane = lax.broadcasted_iota(I32, (8, 128), 1)
    entry = lax.broadcasted_iota(I32, (8, 128), 0)
    for b in range(OWN):
        cut = slice(128 * b, 128 * b + 128)
        f = RATIO * (128 * b + lane) + off[:, cut]
        w = jnp.where(entry < cnt[:, cut], wgt[:, cut], 0.0)
        here = (f >= 0) & (f < FINE)
        fo = jnp.where(here, f, 0)
        f_all[b] = fo
        r_all[b] = fo & (SEG - 1)
        w_all[b] = jnp.where(here, w, 0.0)
        if b < half:
            f_out[b] = jnp.where(f < 0, f + FINE, 0)
            w_out[b] = jnp.where(f < 0, w, 0.0)
        if b >= OWN - half:
            at = b - OWN + 2 * half
            f_out[at] = jnp.where(f >= FINE, f - FINE, 0)
            w_out[at] = jnp.where(f >= FINE, w, 0.0)

    def fetch(b, at):
        return pltpu.make_async_copy(r_all.at[b], slots.at[at], slot_sem.at[at])

    fetch(0, 0).start()
    fetch(1, 1).start()
    up_out[0:1, :] = inc[ROWS - 1 : ROWS, HALO : HALO + COLS]
    up_out[1:2, :] = vc[ROWS - 1 : ROWS, :]
    down_out[...] = inc[0:1, HALO : HALO + COLS]

    pl.semaphore_wait(barrier, len(greeted))

    to_left, to_right = spot(left, slab), spot(right, slab)
    to_lower, to_upper = spot(tile, lower), spot(tile, upper)
    lists = [
        send(f_out.at[0:half], f_for.at[0:half], 0, to_left),
        send(w_out.at[0:half], w_for.at[0:half], 1, to_left),
        send(f_out.at[half : 2 * half], f_for.at[half : 2 * half], 2, to_right),
        send(w_out.at[half : 2 * half], w_for.at[half : 2 * half], 3, to_right),
    ]
    halos = [
        send(inc.at[:, HALO : 2 * HALO], inc.at[:, HALO + COLS : EXT], 4, to_left),
        send(inc.at[:, COLS : COLS + HALO], inc.at[:, 0:HALO], 5, to_right),
        send(up_out, below, 6, to_upper),
        send(down_out, above, 7, to_lower),
    ]

    loads[8].wait()
    loads[9].wait()
    for i in range(M):
        for at, value in ((i, steps[i]), (M + i, grads[i])):
            field = value.astype(F32)
            pairs[at, :, HALO : HALO + COLS] = field
            pair_up[at : at + 1, :] = field[ROWS - 1 : ROWS]
            pair_down[at : at + 1, :] = field[0:1]
    pair_halos = [
        remote(pairs.at[:, :, HALO : 2 * HALO], pairs.at[:, :, HALO + COLS : EXT], 14, to_left),
        remote(pairs.at[:, :, COLS : COLS + HALO], pairs.at[:, :, 0:HALO], 15, to_right),
        remote(pair_up, pair_below, 16, to_upper),
        remote(pair_down, pair_above, 17, to_lower),
    ]

    for copy in cuts:
        copy.wait()
    last = FINE // SEG
    tail = FINE - last * SEG
    for b in range(SEG // 128):
        pieces = [dep[:, SEG * g + 128 * b : SEG * g + 128 * b + 128] for g in range(last)]
        if 128 * b < tail:
            pieces.append(dep[:, SEG * last + 128 * b : SEG * last + 128 * b + 128])
        else:
            pieces.append(jnp.zeros((ROWS, 128), F32))
        fine[128 * b : 128 * b + 128, :] = jnp.concatenate(pieces, axis=0).T

    def gather(at, rows, lanes):
        for u in lanes:
            for k in range(K):
                rows[k * 128 + u : k * 128 + u + 1, :] = fine[pl.ds(slots[at, k, u], 1), :]

    def weighed(b, rows):
        segment = f_all[b] // SEG
        weights = w_all[b]
        chosen = [jnp.where(segment == g, weights, 0.0) for g in range(8)]
        total = jnp.zeros((ROWS, 128), F32)
        for k in range(K):
            flat = rows[128 * k : 128 * k + 128, :].T
            for g in range(8):
                total = total + chosen[g][k : k + 1, :] * flat[ROWS * g : ROWS * g + ROWS]
        return total

    def block_of(i):
        return jnp.where(i < EARLY, 2 * i, jnp.where(i < EARLY + 2, OWN + 2 * (i - EARLY), 2 * (i - 2)))

    edge = OWN + FOREIGN - 1
    turns = (OWN + FOREIGN - 1) // 2

    def pair(i, carry):
        @pl.when(i == EARLY + 2)
        def _():
            fetch(edge, 2).wait()
            gather(2, rows_a, [*range(16), *range(112, 128)])
            far = weighed(edge - 1, rows_b)
            rest = weighed(edge, rows_a)
            at = lax.broadcasted_iota(I32, (ROWS, 128), 1)
            sum_out[0, :, 0:128] = result[OWN]
            sum_out[0, :, 128:256] = result[OWN + 1]
            sum_out[0, :, 256:384] = jnp.where(at < 64, rest, 0.0)
            sum_out[1, :, 0:128] = jnp.where(at < 64, 0.0, rest)
            sum_out[1, :, 128:256] = result[OWN + 2]
            sum_out[1, :, 256:384] = far
            for copy in sums:
                copy.start()

        b = block_of(i)
        before = jnp.where(i == 0, edge + 1, block_of(i - 1) + 1)
        later = jnp.where(i < turns - 1, block_of(i + 1), 0)
        fetch(b, 0).wait()
        gather(0, rows_a, range(128))

        @pl.when(i == EARLY - 1)
        def _():
            for copy in lists:
                copy.wait()
            for copy in pair_halos:
                copy.start()
            for at, b in enumerate((0, 1, 4, 5)):
                f_all[OWN + at] = f_for[b]
                w_all[OWN + at] = w_for[b]
                r_all[OWN + at] = f_for[b] & (SEG - 1)
            f_all[edge] = jnp.where(lane < 64, f_for[2], f_for[3])
            w_all[edge] = jnp.where(lane < 64, w_for[2], w_for[3])
            r_all[edge] = f_all[edge] & (SEG - 1)
            fetch(edge, 2).start()

        fetch(later, 0).start()
        result[before] = weighed(before, rows_b)
        fetch(b + 1, 1).wait()
        gather(1, rows_b, range(128))
        fetch(later + 1, 1).start()
        result[b] = weighed(b, rows_a)
        return carry

    sums = [
        remote(sum_out.at[0], sum_in.at[0], 8, to_right),
        remote(sum_out.at[1], sum_in.at[1], 9, to_left),
    ]
    f_all[edge + 1] = jnp.zeros((K, 128), I32)
    w_all[edge + 1] = jnp.zeros((K, 128), F32)
    rows_b[...] = jnp.zeros((K * 128, 128), F32)
    lax.fori_loop(0, turns, pair, 0)
    fetch(0, 0).wait()
    fetch(1, 1).wait()
    result[OWN - 1] = weighed(OWN - 1, rows_b)

    for i in range(5, 8):
        loads[i].wait()
    spots = (nbr[...] - tile * COLS + HALO) & (tiles * COLS - 1)
    counted = lax.broadcasted_iota(I32, (WIDE, WIDE), 0).astype(F32).astype(BF16)

    def chosen_columns(side, b, t):
        where = spots[2 + side : 3 + side, WIDE * b : WIDE * b + WIDE] - (WIDE * (b + t) + HALO * side)
        where = jnp.where((where >= 0) & (where < WIDE), where, -1).astype(F32)
        hit = counted == jnp.broadcast_to(where, (ROWS, WIDE)).astype(BF16)[0:1, :]
        return jnp.where(hit, jnp.ones((), BF16), jnp.zeros((), BF16))

    for copy in halos:
        copy.wait()
    parts[...] = halves(inc[...])
    mid = inc[:, HALO : HALO + COLS]
    row = lax.broadcasted_iota(I32, (ROWS, COLS), 0)
    couplings = vc[...]
    below_row = jnp.where(slab > 0, below[0:1, :], 0.0)
    below_coupling = jnp.where(slab > 0, below[1:2, :], 0.0)
    above_row = jnp.where(slab < slabs - 1, above[...], 0.0)
    couplings_down = jnp.where(row == 0, below_coupling, pltpu.roll(couplings, 1, 0))

    def vertical(value, under, over):
        up = jnp.where(row == ROWS - 1, over, pltpu.roll(value, ROWS - 1, 0))
        down = jnp.where(row == 0, under, pltpu.roll(value, 1, 0))
        return couplings * up + couplings_down * down

    image = cen[...] * mid + vertical(mid, below_row, above_row)
    near = inc[:, HALO - 128 : HALO + COLS + 128]
    image = image + cpl[0:1, :] * pltpu.roll(near, 1, 1)[:, 128 : 128 + COLS]
    image = image + cpl[1:2, :] * pltpu.roll(near, COLS + 255, 1)[:, 128 : 128 + COLS]
    blocks = []
    for b in range(COLS // WIDE):
        total = None
        for side in range(2):
            got = None
            for t in range(REACH // WIDE):
                start = WIDE * (b + t) + HALO * side
                found = jnp.dot(
                    parts[:, start : start + WIDE], chosen_columns(side, b, t), preferred_element_type=F32
                )
                got = found if got is None else got + found
            term = cpl[2 + side : 3 + side, WIDE * b : WIDE * b + WIDE] * (got[0:ROWS] + got[ROWS : 2 * ROWS])
            total = term if total is None else total + term
        blocks.append(total)
    image = image + jnp.concatenate(blocks, axis=1)

    middle = slice(HALO, HALO + COLS)
    prods[...] = jnp.zeros((128, 128), F32)
    slot = {}
    for i in range(M):
        for j in range(i, M):
            for name, at in (("sy", i), ("yy", M + i)):
                here = slot[name, i, j] = len(slot)
                prods[here : here + 1, :] = lane_sums(pairs[at, :, middle] * pairs[M + j, :, middle])

    for copy in sums:
        copy.wait()
    blank = jnp.zeros((ROWS, COLS - 2 * EDGE), F32)
    restricted = jnp.concatenate([result[b] for b in range(OWN)], axis=1)
    restricted = restricted + jnp.concatenate([sum_in[0], blank, sum_in[1]], axis=1)
    misfit = image - restricted
    mis_out[0] = misfit[ROWS - 1 : ROWS, :]
    mis_out[1] = misfit[0:1, :]
    edges = [
        send(mis_out.at[0], mis_in.at[0], 10, to_upper),
        send(mis_out.at[1], mis_in.at[1], 11, to_lower),
    ]

    spread[...] = jnp.zeros((ROWS, EXT), F32)
    blank = jnp.zeros((ROWS, 128), F32)
    back = jnp.concatenate([blank, cpl[0:1, :] * misfit, blank], axis=1)
    forth = jnp.concatenate([blank, cpl[1:2, :] * misfit, blank], axis=1)
    spread[:, HALO - 128 : HALO + COLS + 128] = pltpu.roll(back, COLS + 255, 1) + pltpu.roll(forth, 1, 1)
    for b in range(COLS // WIDE):
        for side in range(2):
            start = WIDE * b + HALO * side
            carried = halves(cpl[2 + side : 3 + side, WIDE * b : WIDE * b + WIDE] * misfit[:, WIDE * b : WIDE * b + WIDE])
            for t in range(REACH // WIDE):
                out = lax.dot_general(
                    carried, chosen_columns(side, b, t), (((1,), (1,)), ((), ())), preferred_element_type=F32
                )
                at = slice(start + WIDE * t, start + WIDE * t + WIDE)
                spread[:, at] = spread[:, at] + (out[0:ROWS] + out[ROWS : 2 * ROWS])
    rims = [
        send(spread.at[:, 0:HALO], rim_in.at[:, COLS - HALO : COLS], 12, to_left),
        send(spread.at[:, HALO + COLS : EXT], rim_in.at[:, 0:HALO], 13, to_right),
    ]
    part = mid + (cen[...] * misfit + vertical(misfit, 0.0, 0.0) + spread[:, middle])

    for copy in pair_halos:
        copy.wait()
    late = 24
    to_below = below_coupling * misfit[0:1, :]
    to_above = jnp.where(slab < slabs - 1, couplings[ROWS - 1 : ROWS, :] * misfit[ROWS - 1 : ROWS, :], 0.0)
    beyond = lane_blocks(pair_below[...] * to_below + pair_above[...] * to_above)
    sides = []
    for at in range(2 * M):
        total = lane_blocks(pairs[at, :, 0:HALO] * spread[:, 0:HALO])
        total = total + lane_blocks(pairs[at, :, HALO + COLS : EXT] * spread[:, HALO + COLS : EXT])
        total = total + lane_blocks(pairs[at, :, middle] * part)
        sides.append(jnp.sum(total, axis=0, keepdims=True))
        slot["sg" if at < M else "yg", at % M] = late + at
    prods[late : late + 2 * M, :] = jnp.concatenate(sides, axis=0) + beyond

    def finish():
        for copy in edges:
            copy.wait()
        under = jnp.where(slab > 0, mis_in[0], 0.0)
        over = jnp.where(slab < slabs - 1, mis_in[1], 0.0)
        for copy in rims:
            copy.wait()
        whole = part + jnp.where(row == 0, couplings_down * under, 0.0)
        whole = whole + jnp.where(row == ROWS - 1, couplings * over, 0.0)
        gradient[...] = whole + rim_in[...]
        gradient_out.start()

    gradient_out = pltpu.make_async_copy(gradient, gradient_hbm, local_sem.at[11])
    direction_out = pltpu.make_async_copy(direction, direction_hbm, local_sem.at[12])

    def reduced(value, buf, me, peers, sends, recvs, beside=None):
        count = len(peers) + 1
        buf[me] = value
        copies = []
        for d, peer in enumerate(peers):
            copy = pltpu.make_async_remote_copy(
                src_ref=buf.at[me],
                dst_ref=buf.at[me],
                send_sem=sends.at[d],
                recv_sem=recvs.at[d],
                device_id=peer,
                device_id_type=pl.DeviceIdType.MESH,
            )
            copy.start()
            copies.append(copy)
        if beside is not None:
            beside()
        for copy in copies:
            copy.wait()
        total = buf[0]
        for i in range(1, count):
            total = total + buf[i]
        return total

    total = jnp.sum(prods[...].T, axis=0, keepdims=True)
    total = reduced(total, red_plane, row_y * slabs + slab, plane_peers, plane_send, plane_recv)
    total = reduced(total, red_z, row_z, z_peers, z_send, z_recv, finish)

    spreaded = jnp.broadcast_to(total, (128, 128)).T
    of = {name: spreaded[at : at + 1, :] for name, at in slot.items()}
    rho = [1.0 / of["sy", i, i] for i in range(M)]
    alpha = [None] * M
    for i in range(M - 1, -1, -1):
        value = of["sg", i]
        for j in range(i + 1, M):
            value = value - alpha[j] * of["sy", i, j]
        alpha[i] = rho[i] * value
    gamma = of["sy", M - 1, M - 1] / of["yy", M - 1, M - 1]
    keep = []
    for i in range(M):
        value = of["yg", i]
        for j in range(M):
            value = value - alpha[j] * of["yy", min(i, j), max(i, j)]
        value = gamma * value
        for j in range(i):
            value = value + keep[j] * of["sy", j, i]
        keep.append(alpha[i] - rho[i] * value)

    def wide(value):
        return jnp.concatenate([value] * (COLS // 128), axis=1)

    found = wide(-gamma) * gradient[...]
    for i in range(M):
        found = found + wide(gamma * alpha[i]) * pairs[M + i, :, middle]
        found = found - wide(keep[i]) * pairs[i, :, middle]
    direction[...] = found
    direction_out.start()
    gradient_out.wait()
    direction_out.wait()


def hand_over(first, second, first_out, second_out, staged, sem):
    pulls = [pltpu.make_async_copy(ref, staged.at[i], sem.at[i]) for i, ref in enumerate((first, second))]
    pushes = [
        pltpu.make_async_copy(staged.at[i], ref, sem.at[2 + i]) for i, ref in enumerate((first_out, second_out))
    ]
    for copy in pulls:
        copy.start()
    for pull, push in zip(pulls, pushes):
        pull.wait()
        push.start()
    for copy in pushes:
        copy.wait()


def per_device(tiles, slabs, *args):
    (dep, off, wgt, cnt, inc, cen, vc, nbr, cpl, steps, grads) = args
    cnt = cnt.reshape(1, COLS)
    vmem = pltpu.VMEM
    sems = pltpu.SemaphoreType.DMA
    nz = tiles // NY
    shape = jax.ShapeDtypeStruct((ROWS, COLS), F32)
    made = pl.pallas_call(
        functools.partial(kernel, tiles, slabs),
        out_shape=(shape, shape),
        in_specs=[pl.BlockSpec(memory_space=pltpu.HBM)] * 11,
        out_specs=[pl.BlockSpec(memory_space=pltpu.HBM)] * 2,
        scratch_shapes=[
            vmem((ROWS, FINE), F32),
            vmem((K, COLS), I32),
            vmem((K, COLS), F32),
            vmem((1, COLS), I32),
            vmem((ROWS, COLS), F32),
            vmem((ROWS, COLS), F32),
            vmem((4, COLS), I32),
            vmem((4, COLS), F32),
            vmem((M, ROWS, COLS), BF16),
            vmem((M, ROWS, COLS), BF16),
            vmem((SEG, 128), F32),
            vmem((K * 128, 128), F32),
            vmem((K * 128, 128), F32),
            vmem((OWN + FOREIGN + 1, ROWS, 128), F32),
            vmem((OWN + FOREIGN + 1, K, 128), I32),
            vmem((OWN + FOREIGN + 1, K, 128), F32),
            vmem((OWN + FOREIGN, K, 128), I32),
            vmem((2 * EDGE // 128, K, 128), I32),
            vmem((2 * EDGE // 128, K, 128), F32),
            vmem((2 * EDGE // 128, K, 128), I32),
            vmem((2 * EDGE // 128, K, 128), F32),
            pltpu.SMEM((3, K, 128), I32),
            vmem((ROWS, EXT), F32),
            vmem((2 * ROWS, EXT), BF16),
            vmem((2, COLS), F32),
            vmem((2, COLS), F32),
            vmem((1, COLS), F32),
            vmem((1, COLS), F32),
            vmem((2, ROWS, EDGE), F32),
            vmem((2, ROWS, EDGE), F32),
            vmem((2, 1, COLS), F32),
            vmem((2, 1, COLS), F32),
            vmem((ROWS, EXT), F32),
            vmem((ROWS, COLS), F32),
            vmem((2 * M, ROWS, EXT), F32),
            vmem((2 * M, COLS), F32),
            vmem((2 * M, COLS), F32),
            vmem((2 * M, COLS), F32),
            vmem((2 * M, COLS), F32),
            vmem((ROWS, COLS), F32),
            vmem((ROWS, COLS), F32),
            vmem((128, 128), F32),
            vmem((NY * slabs, 1, 128), F32),
            vmem((nz, 1, 128), F32),
            sems((13,)),
            sems((8,)),
            sems((3,)),
            sems((18,)),
            sems((18,)),
            sems((NY * slabs,)),
            sems((NY * slabs,)),
            sems((nz,)),
            sems((nz,)),
        ],
        compiler_params=pltpu.CompilerParams(
            collective_id=0, has_side_effects=True, vmem_limit_bytes=60 * 1024 * 1024
        ),
        cost_estimate=pl.CostEstimate(flops=1 << 28, bytes_accessed=1 << 22, transcendentals=0),
    )(dep, off, wgt, cnt, inc, cen, vc, nbr, cpl, steps, grads)
    return pl.pallas_call(
        hand_over,
        out_shape=(shape, shape),
        in_specs=[pl.BlockSpec(memory_space=pltpu.HBM)] * 2,
        out_specs=[pl.BlockSpec(memory_space=pltpu.HBM)] * 2,
        scratch_shapes=[vmem((2, ROWS, COLS), F32), sems((4,))],
        compiler_params=pltpu.CompilerParams(vmem_limit_bytes=60 * 1024 * 1024),
    )(*made)


def solution(mesh):
    tiles, slabs = mesh.shape["cols"], mesh.shape["lev"]
    return jax.shard_map(
        functools.partial(per_device, tiles, slabs),
        mesh=mesh,
        in_specs=(
            P("lev", "cols"),
            P(None, "cols"),
            P(None, "cols"),
            P("cols"),
            P("lev", "cols"),
            P("lev", "cols"),
            P("lev", "cols"),
            P(None, "cols"),
            P(None, "cols"),
            P(None, "lev", "cols"),
            P(None, "lev", "cols"),
        ),
        out_specs=(P("lev", "cols"), P("lev", "cols")),
        check_vma=False,
    )
```

```python
import functools

import jax
import jax.numpy as jnp
from jax import lax
from jax.experimental import pallas as pl
from jax.experimental.pallas import tpu as pltpu
from jax.sharding import PartitionSpec as P

K = 8
M = 4
RATIO = 31
ROWS = 16
COLS = 1024
FINE = RATIO * COLS
SEG = 4096
HALO = 512
EXT = COLS + 2 * HALO
EDGE = 384
OWN = COLS // 128
FOREIGN = 5
EARLY = 2
WIDE = 256
REACH = WIDE + HALO
NY = 4
F32 = jnp.float32
I32 = jnp.int32
BF16 = jnp.bfloat16


def halves(value):
    high = value.astype(BF16)
    low = (value - high.astype(F32)).astype(BF16)
    return jnp.concatenate([high, low], axis=0)


def lane_blocks(value):
    parts = [value[:, 128 * i : 128 * i + 128] for i in range(value.shape[1] // 128)]
    while len(parts) > 1:
        parts = [parts[i] + parts[i + 1] for i in range(0, len(parts), 2)]
    return parts[0]


def lane_sums(value):
    return jnp.sum(lane_blocks(value[0:8] + value[8:16]), axis=0, keepdims=True)


def kernel(
    tiles,
    slabs,
    dep_hbm,
    off_hbm,
    wgt_hbm,
    cnt_hbm,
    inc_hbm,
    cen_hbm,
    vc_hbm,
    nbr_hbm,
    cpl_hbm,
    step_hbm,
    grad_hbm,
    gradient_hbm,
    direction_hbm,
    dep,
    off,
    wgt,
    cnt,
    cen,
    vc,
    nbr,
    cpl,
    steps,
    grads,
    fine,
    rows_a,
    rows_b,
    result,
    f_all,
    w_all,
    r_all,
    list_out,
    list_in,
    slots,
    inc,
    parts,
    up_out,
    below,
    down_out,
    above,
    sum_out,
    sum_in,
    mis_out,
    mis_in,
    spread,
    rim_in,
    pairs,
    pair_up,
    pair_below,
    pair_down,
    pair_above,
    gradient,
    direction,
    prods,
    red_plane,
    red_z,
    local_sem,
    dep_sem,
    slot_sem,
    send_sem,
    recv_sem,
    plane_send,
    plane_recv,
    z_send,
    z_recv,
):
    tile = lax.axis_index("cols")
    slab = lax.axis_index("lev")
    nz = tiles // NY
    row_z = tile // NY
    row_y = lax.rem(tile, NY)
    left = lax.rem(tile + tiles - 1, tiles)
    right = lax.rem(tile + 1, tiles)
    lower = lax.rem(slab + slabs - 1, slabs)
    upper = lax.rem(slab + 1, slabs)

    def spot(column, level):
        return {"cols": column, "lev": level}

    def around(count):
        return sorted(range(1, count), key=lambda d: -min(d, count - d))

    plane_peers = [
        spot(row_z * NY + lax.rem(row_y + e, NY), lax.rem(slab + d, slabs))
        for e in around(NY) + [0]
        for d in around(slabs) + [0]
        if d or e
    ]
    z_peers = [spot(lax.rem(row_z + d, nz) * NY + row_y, slab) for d in around(nz)]

    def remote(src, dst, i, target):
        return pltpu.make_async_remote_copy(
            src_ref=src,
            dst_ref=dst,
            send_sem=send_sem.at[i],
            recv_sem=recv_sem.at[i],
            device_id=target,
            device_id_type=pl.DeviceIdType.MESH,
        )

    def send(src, dst, i, target):
        copy = remote(src, dst, i, target)
        copy.start()
        return copy

    barrier = pltpu.get_barrier_semaphore()
    greeted = [spot(left, slab), spot(right, slab)] + plane_peers + z_peers
    for peer in greeted:
        pl.semaphore_signal(barrier, inc=1, device_id=peer, device_id_type=pl.DeviceIdType.MESH)

    loads, cuts = [], []
    for i, (src, dst) in enumerate(
        [
            (off_hbm, off),
            (wgt_hbm, wgt),
            (cnt_hbm, cnt),
            (inc_hbm, inc.at[:, HALO : HALO + COLS]),
            (vc_hbm, vc),
            (nbr_hbm, nbr),
            (cpl_hbm, cpl),
            (cen_hbm, cen),
            (step_hbm, steps),
            (grad_hbm, grads),
        ]
    ):
        copy = pltpu.make_async_copy(src, dst, local_sem.at[i])
        copy.start()
        loads.append(copy)
        if i == 4:
            for g in range(8):
                part = slice(SEG * g, min(SEG * g + SEG, FINE))
                copy = pltpu.make_async_copy(dep_hbm.at[:, part], dep.at[:, part], dep_sem.at[g])
                copy.start()
                cuts.append(copy)

    for i in range(5):
        loads[i].wait()

    half = EDGE // 128
    lane = lax.broadcasted_iota(I32, (8, 128), 1)
    entry = lax.broadcasted_iota(I32, (8, 128), 0)
    for b in range(OWN):
        cut = slice(128 * b, 128 * b + 128)
        f = RATIO * (128 * b + lane) + off[:, cut]
        w = jnp.where(entry < cnt[:, cut], wgt[:, cut], 0.0)
        here = (f >= 0) & (f < FINE)
        fo = jnp.where(here, f, 0)
        f_all[b] = fo
        r_all[b] = fo & (SEG - 1)
        w_all[b] = jnp.where(here, w, 0.0)
        if b < half:
            list_out[b, 0:K] = jnp.where(f < 0, f + FINE, 0).astype(F32)
            list_out[b, K : 2 * K] = jnp.where(f < 0, w, 0.0)
        if b >= OWN - half:
            at = b - OWN + 2 * half
            list_out[at, 0:K] = jnp.where(f >= FINE, f - FINE, 0).astype(F32)
            list_out[at, K : 2 * K] = jnp.where(f >= FINE, w, 0.0)

    def fetch(b, at):
        return pltpu.make_async_copy(r_all.at[b], slots.at[at], slot_sem.at[at])

    fetch(0, 0).start()
    fetch(1, 1).start()
    up_out[0:1, :] = inc[ROWS - 1 : ROWS, HALO : HALO + COLS]
    up_out[1:2, :] = vc[ROWS - 1 : ROWS, :]
    down_out[...] = inc[0:1, HALO : HALO + COLS]

    pl.semaphore_wait(barrier, len(greeted))

    to_left, to_right = spot(left, slab), spot(right, slab)
    to_lower, to_upper = spot(tile, lower), spot(tile, upper)
    lists = [
        send(list_out.at[0:half], list_in.at[0:half], 0, to_left),
        send(list_out.at[half : 2 * half], list_in.at[half : 2 * half], 1, to_right),
    ]
    halos = [
        send(inc.at[:, HALO : 2 * HALO], inc.at[:, HALO + COLS : EXT], 4, to_left),
        send(inc.at[:, COLS : COLS + HALO], inc.at[:, 0:HALO], 5, to_right),
        send(up_out, below, 6, to_upper),
        send(down_out, above, 7, to_lower),
    ]

    loads[8].wait()
    loads[9].wait()
    for i in range(M):
        for at, value in ((i, steps[i]), (M + i, grads[i])):
            field = value.astype(F32)
            pairs[at, :, HALO : HALO + COLS] = field
            pair_up[at : at + 1, :] = field[ROWS - 1 : ROWS]
            pair_down[at : at + 1, :] = field[0:1]
    pair_halos = [
        remote(pairs.at[:, :, HALO : 2 * HALO], pairs.at[:, :, HALO + COLS : EXT], 14, to_left),
        remote(pairs.at[:, :, COLS : COLS + HALO], pairs.at[:, :, 0:HALO], 15, to_right),
        remote(pair_up, pair_below, 16, to_upper),
        remote(pair_down, pair_above, 17, to_lower),
    ]

    for copy in cuts:
        copy.wait()
    last = FINE // SEG
    tail = FINE - last * SEG
    for b in range(SEG // 128):
        pieces = [dep[:, SEG * g + 128 * b : SEG * g + 128 * b + 128] for g in range(last)]
        if 128 * b < tail:
            pieces.append(dep[:, SEG * last + 128 * b : SEG * last + 128 * b + 128])
        else:
            pieces.append(jnp.zeros((ROWS, 128), F32))
        fine[128 * b : 128 * b + 128, :] = jnp.concatenate(pieces, axis=0).T

    def gather(at, rows, lanes):
        for u in lanes:
            for k in range(K):
                rows[k * 128 + u : k * 128 + u + 1, :] = fine[pl.ds(slots[at, k, u], 1), :]

    def weighed(b, rows):
        segment = f_all[b] // SEG
        weights = w_all[b]
        chosen = [jnp.where(segment == g, weights, 0.0) for g in range(8)]
        total = jnp.zeros((ROWS, 128), F32)
        for k in range(K):
            flat = rows[128 * k : 128 * k + 128, :].T
            for g in range(8):
                total = total + chosen[g][k : k + 1, :] * flat[ROWS * g : ROWS * g + ROWS]
        return total

    def block_of(i):
        return jnp.where(i < EARLY, 2 * i, jnp.where(i < EARLY + 2, OWN + 2 * (i - EARLY), 2 * (i - 2)))

    edge = OWN + FOREIGN - 1
    turns = (OWN + FOREIGN - 1) // 2

    def pair(i, carry):
        @pl.when(i == EARLY + 2)
        def _():
            fetch(edge, 2).wait()
            gather(2, rows_a, [*range(16), *range(112, 128)])
            far = weighed(edge - 1, rows_b)
            rest = weighed(edge, rows_a)
            at = lax.broadcasted_iota(I32, (ROWS, 128), 1)
            sum_out[0, :, 0:128] = result[OWN]
            sum_out[0, :, 128:256] = result[OWN + 1]
            sum_out[0, :, 256:384] = jnp.where(at < 64, rest, 0.0)
            sum_out[1, :, 0:128] = jnp.where(at < 64, 0.0, rest)
            sum_out[1, :, 128:256] = result[OWN + 2]
            sum_out[1, :, 256:384] = far
            for copy in sums:
                copy.start()

        b = block_of(i)
        before = jnp.where(i == 0, edge + 1, block_of(i - 1) + 1)
        later = jnp.where(i < turns - 1, block_of(i + 1), 0)
        fetch(b, 0).wait()
        gather(0, rows_a, range(128))

        @pl.when(i == EARLY - 1)
        def _():
            for copy in lists:
                copy.wait()
            for copy in pair_halos:
                copy.start()
            for at, b in enumerate((0, 1, 4, 5)):
                f_all[OWN + at] = list_in[b, 0:K].astype(I32)
                w_all[OWN + at] = list_in[b, K : 2 * K]
                r_all[OWN + at] = f_all[OWN + at] & (SEG - 1)
            f_all[edge] = jnp.where(lane < 64, list_in[2, 0:K], list_in[3, 0:K]).astype(I32)
            w_all[edge] = jnp.where(lane < 64, list_in[2, K : 2 * K], list_in[3, K : 2 * K])
            r_all[edge] = f_all[edge] & (SEG - 1)
            fetch(edge, 2).start()

        fetch(later, 0).start()
        result[before] = weighed(before, rows_b)
        fetch(b + 1, 1).wait()
        gather(1, rows_b, range(128))
        fetch(later + 1, 1).start()
        result[b] = weighed(b, rows_a)
        return carry

    sums = [
        remote(sum_out.at[0], sum_in.at[0], 8, to_right),
        remote(sum_out.at[1], sum_in.at[1], 9, to_left),
    ]
    f_all[edge + 1] = jnp.zeros((K, 128), I32)
    w_all[edge + 1] = jnp.zeros((K, 128), F32)
    rows_b[...] = jnp.zeros((K * 128, 128), F32)
    lax.fori_loop(0, turns, pair, 0)
    fetch(0, 0).wait()
    fetch(1, 1).wait()
    result[OWN - 1] = weighed(OWN - 1, rows_b)

    for i in range(5, 8):
        loads[i].wait()
    spots = (nbr[...] - tile * COLS + HALO) & (tiles * COLS - 1)
    counted = lax.broadcasted_iota(I32, (WIDE, WIDE), 0).astype(F32).astype(BF16)

    def chosen_columns(side, b, t):
        where = spots[2 + side : 3 + side, WIDE * b : WIDE * b + WIDE] - (WIDE * (b + t) + HALO * side)
        where = jnp.where((where >= 0) & (where < WIDE), where, -1).astype(F32)
        hit = counted == jnp.broadcast_to(where, (ROWS, WIDE)).astype(BF16)[0:1, :]
        return jnp.where(hit, jnp.ones((), BF16), jnp.zeros((), BF16))

    for copy in halos:
        copy.wait()
    parts[...] = halves(inc[...])
    mid = inc[:, HALO : HALO + COLS]
    row = lax.broadcasted_iota(I32, (ROWS, COLS), 0)
    couplings = vc[...]
    below_row = jnp.where(slab > 0, below[0:1, :], 0.0)
    below_coupling = jnp.where(slab > 0, below[1:2, :], 0.0)
    above_row = jnp.where(slab < slabs - 1, above[...], 0.0)
    couplings_down = jnp.where(row == 0, below_coupling, pltpu.roll(couplings, 1, 0))

    def vertical(value, under, over):
        up = jnp.where(row == ROWS - 1, over, pltpu.roll(value, ROWS - 1, 0))
        down = jnp.where(row == 0, under, pltpu.roll(value, 1, 0))
        return couplings * up + couplings_down * down

    image = cen[...] * mid + vertical(mid, below_row, above_row)
    near = inc[:, HALO - 128 : HALO + COLS + 128]
    image = image + cpl[0:1, :] * pltpu.roll(near, 1, 1)[:, 128 : 128 + COLS]
    image = image + cpl[1:2, :] * pltpu.roll(near, COLS + 255, 1)[:, 128 : 128 + COLS]
    blocks = []
    for b in range(COLS // WIDE):
        total = None
        for side in range(2):
            got = None
            for t in range(REACH // WIDE):
                start = WIDE * (b + t) + HALO * side
                found = jnp.dot(
                    parts[:, start : start + WIDE], chosen_columns(side, b, t), preferred_element_type=F32
                )
                got = found if got is None else got + found
            term = cpl[2 + side : 3 + side, WIDE * b : WIDE * b + WIDE] * (got[0:ROWS] + got[ROWS : 2 * ROWS])
            total = term if total is None else total + term
        blocks.append(total)
    image = image + jnp.concatenate(blocks, axis=1)

    middle = slice(HALO, HALO + COLS)
    prods[...] = jnp.zeros((128, 128), F32)
    slot = {}
    for i in range(M):
        for j in range(i, M):
            for name, at in (("sy", i), ("yy", M + i)):
                here = slot[name, i, j] = len(slot)
                prods[here : here + 1, :] = lane_sums(pairs[at, :, middle] * pairs[M + j, :, middle])

    for copy in sums:
        copy.wait()
    blank = jnp.zeros((ROWS, COLS - 2 * EDGE), F32)
    restricted = jnp.concatenate([result[b] for b in range(OWN)], axis=1)
    restricted = restricted + jnp.concatenate([sum_in[0], blank, sum_in[1]], axis=1)
    misfit = image - restricted
    mis_out[0] = misfit[ROWS - 1 : ROWS, :]
    mis_out[1] = misfit[0:1, :]
    edges = [
        send(mis_out.at[0], mis_in.at[0], 10, to_upper),
        send(mis_out.at[1], mis_in.at[1], 11, to_lower),
    ]

    spread[...] = jnp.zeros((ROWS, EXT), F32)
    blank = jnp.zeros((ROWS, 128), F32)
    back = jnp.concatenate([blank, cpl[0:1, :] * misfit, blank], axis=1)
    forth = jnp.concatenate([blank, cpl[1:2, :] * misfit, blank], axis=1)
    spread[:, HALO - 128 : HALO + COLS + 128] = pltpu.roll(back, COLS + 255, 1) + pltpu.roll(forth, 1, 1)
    for b in range(COLS // WIDE):
        for side in range(2):
            start = WIDE * b + HALO * side
            carried = halves(cpl[2 + side : 3 + side, WIDE * b : WIDE * b + WIDE] * misfit[:, WIDE * b : WIDE * b + WIDE])
            for t in range(REACH // WIDE):
                out = lax.dot_general(
                    carried, chosen_columns(side, b, t), (((1,), (1,)), ((), ())), preferred_element_type=F32
                )
                at = slice(start + WIDE * t, start + WIDE * t + WIDE)
                spread[:, at] = spread[:, at] + (out[0:ROWS] + out[ROWS : 2 * ROWS])
    rims = [
        send(spread.at[:, 0:HALO], rim_in.at[:, COLS - HALO : COLS], 12, to_left),
        send(spread.at[:, HALO + COLS : EXT], rim_in.at[:, 0:HALO], 13, to_right),
    ]
    part = mid + (cen[...] * misfit + vertical(misfit, 0.0, 0.0) + spread[:, middle])

    for copy in pair_halos:
        copy.wait()
    late = 24
    to_below = below_coupling * misfit[0:1, :]
    to_above = jnp.where(slab < slabs - 1, couplings[ROWS - 1 : ROWS, :] * misfit[ROWS - 1 : ROWS, :], 0.0)
    beyond = lane_blocks(pair_below[...] * to_below + pair_above[...] * to_above)
    sides = []
    for at in range(2 * M):
        total = lane_blocks(pairs[at, :, 0:HALO] * spread[:, 0:HALO])
        total = total + lane_blocks(pairs[at, :, HALO + COLS : EXT] * spread[:, HALO + COLS : EXT])
        total = total + lane_blocks(pairs[at, :, middle] * part)
        sides.append(jnp.sum(total, axis=0, keepdims=True))
        slot["sg" if at < M else "yg", at % M] = late + at
    prods[late : late + 2 * M, :] = jnp.concatenate(sides, axis=0) + beyond

    def finish():
        for copy in edges:
            copy.wait()
        under = jnp.where(slab > 0, mis_in[0], 0.0)
        over = jnp.where(slab < slabs - 1, mis_in[1], 0.0)
        for copy in rims:
            copy.wait()
        whole = part + jnp.where(row == 0, couplings_down * under, 0.0)
        whole = whole + jnp.where(row == ROWS - 1, couplings * over, 0.0)
        gradient[...] = whole + rim_in[...]
        gradient_out.start()

    gradient_out = pltpu.make_async_copy(gradient, gradient_hbm, local_sem.at[11])
    direction_out = pltpu.make_async_copy(direction, direction_hbm, local_sem.at[12])

    def reduced(value, buf, me, peers, sends, recvs, beside=None):
        count = len(peers) + 1
        buf[me] = value
        copies = []
        for d, peer in enumerate(peers):
            copy = pltpu.make_async_remote_copy(
                src_ref=buf.at[me],
                dst_ref=buf.at[me],
                send_sem=sends.at[d],
                recv_sem=recvs.at[d],
                device_id=peer,
                device_id_type=pl.DeviceIdType.MESH,
            )
            copy.start()
            copies.append(copy)
        if beside is not None:
            beside()
        for copy in copies:
            copy.wait()
        total = buf[0]
        for i in range(1, count):
            total = total + buf[i]
        return total

    total = jnp.sum(prods[...].T, axis=0, keepdims=True)
    total = reduced(total, red_plane, row_y * slabs + slab, plane_peers, plane_send, plane_recv)
    total = reduced(total, red_z, row_z, z_peers, z_send, z_recv, finish)

    spreaded = jnp.broadcast_to(total, (128, 128)).T
    of = {name: spreaded[at : at + 1, :] for name, at in slot.items()}
    rho = [1.0 / of["sy", i, i] for i in range(M)]
    alpha = [None] * M
    for i in range(M - 1, -1, -1):
        value = of["sg", i]
        for j in range(i + 1, M):
            value = value - alpha[j] * of["sy", i, j]
        alpha[i] = rho[i] * value
    gamma = of["sy", M - 1, M - 1] / of["yy", M - 1, M - 1]
    keep = []
    for i in range(M):
        value = of["yg", i]
        for j in range(M):
            value = value - alpha[j] * of["yy", min(i, j), max(i, j)]
        value = gamma * value
        for j in range(i):
            value = value + keep[j] * of["sy", j, i]
        keep.append(alpha[i] - rho[i] * value)

    def wide(value):
        return jnp.concatenate([value] * (COLS // 128), axis=1)

    found = wide(-gamma) * gradient[...]
    for i in range(M):
        found = found + wide(gamma * alpha[i]) * pairs[M + i, :, middle]
        found = found - wide(keep[i]) * pairs[i, :, middle]
    direction[...] = found
    direction_out.start()
    gradient_out.wait()
    direction_out.wait()


def hand_over(first, second, first_out, second_out, staged, sem):
    pulls = [pltpu.make_async_copy(ref, staged.at[i], sem.at[i]) for i, ref in enumerate((first, second))]
    pushes = [
        pltpu.make_async_copy(staged.at[i], ref, sem.at[2 + i]) for i, ref in enumerate((first_out, second_out))
    ]
    for copy in pulls:
        copy.start()
    for pull, push in zip(pulls, pushes):
        pull.wait()
        push.start()
    for copy in pushes:
        copy.wait()


def per_device(tiles, slabs, *args):
    (dep, off, wgt, cnt, inc, cen, vc, nbr, cpl, steps, grads) = args
    cnt = cnt.reshape(1, COLS)
    vmem = pltpu.VMEM
    sems = pltpu.SemaphoreType.DMA
    nz = tiles // NY
    shape = jax.ShapeDtypeStruct((ROWS, COLS), F32)
    made = pl.pallas_call(
        functools.partial(kernel, tiles, slabs),
        out_shape=(shape, shape),
        in_specs=[pl.BlockSpec(memory_space=pltpu.HBM)] * 11,
        out_specs=[pl.BlockSpec(memory_space=pltpu.HBM)] * 2,
        scratch_shapes=[
            vmem((ROWS, FINE), F32),
            vmem((K, COLS), I32),
            vmem((K, COLS), F32),
            vmem((1, COLS), I32),
            vmem((ROWS, COLS), F32),
            vmem((ROWS, COLS), F32),
            vmem((4, COLS), I32),
            vmem((4, COLS), F32),
            vmem((M, ROWS, COLS), BF16),
            vmem((M, ROWS, COLS), BF16),
            vmem((SEG, 128), F32),
            vmem((K * 128, 128), F32),
            vmem((K * 128, 128), F32),
            vmem((OWN + FOREIGN + 1, ROWS, 128), F32),
            vmem((OWN + FOREIGN + 1, K, 128), I32),
            vmem((OWN + FOREIGN + 1, K, 128), F32),
            vmem((OWN + FOREIGN, K, 128), I32),
            vmem((2 * EDGE // 128, 2 * K, 128), F32),
            vmem((2 * EDGE // 128, 2 * K, 128), F32),
            pltpu.SMEM((3, K, 128), I32),
            vmem((ROWS, EXT), F32),
            vmem((2 * ROWS, EXT), BF16),
            vmem((2, COLS), F32),
            vmem((2, COLS), F32),
            vmem((1, COLS), F32),
            vmem((1, COLS), F32),
            vmem((2, ROWS, EDGE), F32),
            vmem((2, ROWS, EDGE), F32),
            vmem((2, 1, COLS), F32),
            vmem((2, 1, COLS), F32),
            vmem((ROWS, EXT), F32),
            vmem((ROWS, COLS), F32),
            vmem((2 * M, ROWS, EXT), F32),
            vmem((2 * M, COLS), F32),
            vmem((2 * M, COLS), F32),
            vmem((2 * M, COLS), F32),
            vmem((2 * M, COLS), F32),
            vmem((ROWS, COLS), F32),
            vmem((ROWS, COLS), F32),
            vmem((128, 128), F32),
            vmem((NY * slabs, 1, 128), F32),
            vmem((nz, 1, 128), F32),
            sems((13,)),
            sems((8,)),
            sems((3,)),
            sems((18,)),
            sems((18,)),
            sems((NY * slabs,)),
            sems((NY * slabs,)),
            sems((nz,)),
            sems((nz,)),
        ],
        compiler_params=pltpu.CompilerParams(
            collective_id=0, has_side_effects=True, vmem_limit_bytes=60 * 1024 * 1024
        ),
        cost_estimate=pl.CostEstimate(flops=1 << 28, bytes_accessed=1 << 22, transcendentals=0),
    )(dep, off, wgt, cnt, inc, cen, vc, nbr, cpl, steps, grads)
    return pl.pallas_call(
        hand_over,
        out_shape=(shape, shape),
        in_specs=[pl.BlockSpec(memory_space=pltpu.HBM)] * 2,
        out_specs=[pl.BlockSpec(memory_space=pltpu.HBM)] * 2,
        scratch_shapes=[vmem((2, ROWS, COLS), F32), sems((4,))],
        compiler_params=pltpu.CompilerParams(vmem_limit_bytes=60 * 1024 * 1024),
    )(*made)


def solution(mesh):
    tiles, slabs = mesh.shape["cols"], mesh.shape["lev"]
    return jax.shard_map(
        functools.partial(per_device, tiles, slabs),
        mesh=mesh,
        in_specs=(
            P("lev", "cols"),
            P(None, "cols"),
            P(None, "cols"),
            P("cols"),
            P("lev", "cols"),
            P("lev", "cols"),
            P("lev", "cols"),
            P(None, "cols"),
            P(None, "cols"),
            P(None, "lev", "cols"),
            P(None, "lev", "cols"),
        ),
        out_specs=(P("lev", "cols"), P("lev", "cols")),
        check_vma=False,
    )
```
